128 devices in a mesh: tile: 16 (over y, x), chan: 8 (over z, core).
Axes of the slice: x: 4, y: 4, z: 4, core: 2. Of those that a mesh axis runs over, the one named last changes fastest.
Arguments:
- latents: bfloat16 [16, 16, 8, 128], P('tile'), may hold values from -6 to 6
- durations: int32 [16], replicated, may hold values from 4 to 8
- assignment: int32 [16], replicated, may hold values from 0 to 15, each once
- entry_weight: bfloat16 [27, 512, 16], P(None, 'chan'), may hold values from -0.3125 to 0.3125
- entry_bias: float32 [512], P('chan'), may hold values from -1 to 1
- first_gain: float32 [512], P('chan'), may hold values from 0.4 to 1.6
- first_shift: float32 [512], P('chan'), may hold values from -0.5 to 0.5
- mixer_weight: bfloat16 [27, 512, 512], P(None, 'chan'), may hold values from -0.0546875 to 0.0546875
- mixer_bias: float32 [512], P('chan'), may hold values from -1 to 1
- second_gain: float32 [512], P('chan'), may hold values from 0.4 to 1.6
- second_shift: float32 [512], P('chan'), may hold values from -0.5 to 0.5
Outputs:
- decoded_frames: bfloat16 [16, 512, 8, 512], P('tile', 'chan')
The draws below stay inside these ranges and needn't reach their ends.
Inputs may be any that keep to these rules, and one draw needn't show every extreme that they name: `assignment`: each tile number appears exactly once.
All inputs are finite; a program needn't handle non-finite values.
Results may differ from the reference program's by a relative error of at most 0.005.
Values may be sent and summed in bfloat16 or wider, within the bound.
A program may use at most 128 MiB of HBM per device.

```python
import jax
import jax.numpy as jnp
from jax import lax

C = 512
CL = 16
GSIZE = 16
FT = 8
HT = 8
WT = 16
OV = 3
TILES = 16


def plant(drawn, rng, low, largest):
    index_at = [jax.random.randint(jax.random.fold_in(rng, axis), (), 0, length) for axis, length in enumerate(drawn.shape)]
    main_axis = drawn.shape.index(max(drawn.shape))
    next_to = index_at[:main_axis] + [(index_at[main_axis] + 1) % drawn.shape[main_axis]] + index_at[main_axis + 1:]
    return drawn.at[tuple(index_at)].set(low).at[tuple(next_to)].set(largest)


def levels(rng, extent, cuts, smallest, largest):
    def one(dim, parts):
        steps = jax.random.uniform(jax.random.fold_in(jax.random.fold_in(rng, 6), dim), (parts,), jnp.float32, smallest / len(cuts), largest / len(cuts))
        return jnp.repeat(jnp.exp(steps), extent[dim] // parts).reshape((-1,) + (1,) * (len(extent) - dim - 1))

    factor_of = one(*cuts[0])
    for cut in cuts[1:]:
        factor_of = factor_of * one(*cut)
    return factor_of


def scatter_about(key, shape, spread, reach, shards=(), kind=jnp.bfloat16):
    drawn = spread * jax.random.normal(key, shape, jnp.float32)
    if shards:
        drawn = drawn * levels(key, shape, shards, -0.22, 0.18)
    return jnp.clip(drawn, -reach, reach).astype(kind)


def setup_inputs(seed: int = 0) -> dict:
    keys = jax.random.split(jax.random.key(seed), 12)
    latents = scatter_about(keys[0], (TILES, CL, FT, HT * WT), 1.0, 6.0, ((0, 16),))
    durations = plant(jax.random.randint(keys[1], (TILES,), OV + 1, FT + 1), jax.random.fold_in(keys[1], 1), OV + 1, FT).astype(jnp.int32)
    assignment = jax.random.permutation(keys[2], TILES).astype(jnp.int32)
    entry_weight = scatter_about(keys[3], (27, C, CL), (27 * CL) ** -0.5, 0.3125, ((1, 8),))
    entry_bias = jnp.clip(jax.random.uniform(keys[4], (C,), jnp.float32, -1.0, 1.0) * levels(keys[4], (C,), ((0, 8),), -0.4, 0.0), -1.0, 1.0)
    first_gain = jnp.clip(1.0 + 0.12 * jax.random.normal(keys[5], (C,), jnp.float32), 0.4, 1.6)
    first_shift = jnp.clip(jax.random.uniform(keys[6], (C,), jnp.float32, -0.5, 0.5) * levels(keys[6], (C,), ((0, 8),), -0.4, 0.0), -0.5, 0.5)
    mixer_weight = scatter_about(keys[7], (27, C, C), (27 * C) ** -0.5, 0.0546875, ((1, 8),))
    mixer_bias = jnp.clip(jax.random.uniform(keys[8], (C,), jnp.float32, -1.0, 1.0) * levels(keys[8], (C,), ((0, 8),), -0.4, 0.0), -1.0, 1.0)
    second_gain = jnp.clip(1.0 + 0.12 * jax.random.normal(keys[9], (C,), jnp.float32), 0.4, 1.6)
    second_shift = jnp.clip(jax.random.uniform(keys[10], (C,), jnp.float32, -0.5, 0.5) * levels(keys[10], (C,), ((0, 8),), -0.4, 0.0), -0.5, 0.5)
    return dict(latents=latents, durations=durations, assignment=assignment, entry_weight=entry_weight, entry_bias=entry_bias, first_gain=first_gain, first_shift=first_shift, mixer_weight=mixer_weight, mixer_bias=mixer_bias, second_gain=second_gain, second_shift=second_shift)


def shifted_sum(stacked, height, width):
    tap_count, channels, frames, cell_count = stacked.shape
    column = jnp.arange(cell_count, dtype=jnp.int32) % width
    summed = jnp.zeros((channels, frames, cell_count), jnp.float32)
    tap_number = 0
    for step_time in range(3):
        for step_row in (-1, 0, 1):
            for step_col in (-1, 0, 1):
                tap_plane = stacked[tap_number]
                delay_frames = 2 - step_time
                if delay_frames > 0:
                    repeated = jnp.repeat(tap_plane[:, :1], delay_frames, axis=1)
                    tap_plane = jnp.concatenate([repeated, tap_plane[:, :frames - delay_frames]], axis=1)
                offset = step_row * width + step_col
                padded = jnp.pad(tap_plane, ((0, 0), (0, 0), (width + 1, width + 1)))
                shifted = padded[:, :, width + 1 + offset:width + 1 + offset + cell_count]
                inside = (column + step_col >= 0) & (column + step_col < width)
                summed = summed + jnp.where(inside, shifted, 0.0)
                tap_number += 1
    return summed

def convolve(inputs, weight, height, width):
    tap_count, out_channels, in_channels = weight.shape
    frames = inputs.shape[1]
    cell_count = inputs.shape[2]
    stacked = jnp.dot(weight.reshape(tap_count * out_channels, in_channels), inputs.reshape(in_channels, frames * cell_count), preferred_element_type=jnp.float32)
    return shifted_sum(stacked.reshape(tap_count, out_channels, frames, cell_count), height, width)

def group_norm(values, gain, shift, duration, group_size):
    channels, frames, cell_count = values.shape
    grouped = values.reshape(channels // group_size, group_size, frames, cell_count)
    live_mask = (jnp.arange(frames, dtype=jnp.int32) < duration).astype(jnp.float32)[None, None, :, None]
    members = group_size * cell_count * duration.astype(jnp.float32)
    average = lax.optimization_barrier(jnp.sum(grouped * live_mask, axis=(1, 2, 3), keepdims=True)) / members
    centred = grouped - average
    variance = lax.optimization_barrier(jnp.sum(centred * centred * live_mask, axis=(1, 2, 3), keepdims=True)) / members
    normed = (centred * lax.rsqrt(variance + 1e-06)).reshape(channels, frames, cell_count)
    return normed * gain[:, None, None] + shift[:, None, None]

def upsample(values, height, width):
    leading = values.shape[:-1]
    expanded = values.reshape(leading + (height, 1, width, 1))
    expanded = jnp.broadcast_to(expanded, leading + (height, 2, width, 2))
    return expanded.reshape(leading + (4 * height * width,))

def reference(latents, durations, assignment, entry_weight, entry_bias, first_gain, first_shift, mixer_weight, mixer_bias, second_gain, second_shift):

    def one_tile(tile_pair):
        latent, duration = tile_pair
        entry_conv = convolve(latent, entry_weight, HT, WT) + entry_bias[:, None, None]
        coarse = jax.nn.silu(group_norm(entry_conv, first_gain, first_shift, duration, GSIZE)).astype(jnp.bfloat16)
        fine_grid = upsample(coarse, HT, WT)
        mixed = convolve(fine_grid, mixer_weight, 2 * HT, 2 * WT) + mixer_bias[:, None, None]
        result = jax.nn.silu(group_norm(mixed, second_gain, second_shift, duration, GSIZE))
        live_frames = (jnp.arange(FT, dtype=jnp.int32) < duration)[None, :, None]
        return jnp.where(live_frames, result, 0.0).astype(jnp.bfloat16)
    decoded_own = lax.map(one_tile, (latents, durations))

    def tail_of(decoded_block, start_frame):
        return lax.dynamic_slice_in_dim(decoded_block, start_frame, OV, axis=1)
    starts = (durations - OV).astype(jnp.int32)
    tail_blocks = jax.vmap(tail_of)(decoded_own, starts)
    previous = jnp.concatenate([tail_blocks[:1], tail_blocks[:-1]], axis=0)
    ramp_weights = ((jnp.arange(OV, dtype=jnp.float32) + 1.0) / (OV + 1.0))[None, None, :, None]
    head_frames = decoded_own[:, :, :OV].astype(jnp.float32)
    blended = head_frames * ramp_weights + previous.astype(jnp.float32) * (1.0 - ramp_weights)
    is_first = (jnp.arange(TILES, dtype=jnp.int32) == 0)[:, None, None, None]
    head_result = jnp.where(is_first, head_frames, blended).astype(jnp.bfloat16)
    assembled = jnp.concatenate([head_result, decoded_own[:, :, OV:]], axis=2)
    return jnp.take(assembled, assignment, axis=0)
```

```python
import functools

import jax
import jax.numpy as jnp
from jax import lax
from jax.experimental import pallas as pl
from jax.experimental.pallas import tpu as pltpu
from jax.sharding import PartitionSpec as P

MESH = pl.DeviceIdType.MESH
GSIZE = 16
OV = 3
FT = 8
WT = 16
CELLS = 128
CL = 16
COUT = 64
CIN = 512
KE = 512
WROWS = 432
EPS = 1e-06


def three_parts(x):
    hi = x.astype(jnp.bfloat16).astype(jnp.float32)
    rest = x - hi
    mid = rest.astype(jnp.bfloat16).astype(jnp.float32)
    return hi, mid, rest - mid


def gather_kernel(
    tiles, chans,
    assign, lat, wt, bias, gain, shift,
    we, sel,
    ext, stage,
    s_lat, r_lat, s_z, r_z, s_sib, r_sib, s_sel, r_sel,
):
    me_t = lax.axis_index("tile")
    me_c = lax.axis_index("chan")
    z, core = me_c // 2, me_c % 2

    barrier = pltpu.get_barrier_semaphore()
    for d in range(1, tiles):
        pl.semaphore_signal(barrier, inc=1, device_id=((me_t + d) % tiles, me_c), device_id_type=MESH)
    for d in range(1, chans):
        pl.semaphore_signal(barrier, inc=1, device_id=(me_t, (me_c + d) % chans), device_id_type=MESH)

    ext[:WROWS, :] = wt[...]
    row = lax.broadcasted_iota(jnp.int32, (16, COUT), 0)
    packed = jnp.zeros((16, COUT), jnp.float32)
    for base, ref in ((0, bias), (3, gain), (6, shift)):
        for at, part in enumerate(three_parts(ref[...])):
            packed = jnp.where(row == base + at, part, packed)
    ext[WROWS:WROWS + 16, :] = packed.astype(jnp.bfloat16)
    ext[WROWS + 16:, :] = jnp.zeros((KE - WROWS - 16, COUT), jnp.bfloat16)
    eye = (
        lax.broadcasted_iota(jnp.int32, (COUT, COUT), 0)
        == lax.broadcasted_iota(jnp.int32, (COUT, COUT), 1)
    ).astype(jnp.bfloat16)
    mine = pl.ds(pl.multiple_of(me_c * COUT, COUT), COUT)
    we[mine, :] = lax.dot_general(
        eye, ext[...], (((1,), (1,)), ((), ())), preferred_element_type=jnp.float32
    ).astype(jnp.bfloat16)
    part_rows = CL // chans
    stage[me_t] = lat[pl.ds(me_c * part_rows, part_rows)]

    pl.semaphore_wait(barrier, tiles + chans - 2)

    lat_copies = []
    for d in range(1, tiles):
        copy = pltpu.make_async_remote_copy(
            src_ref=lat.at[pl.ds(me_c * part_rows, part_rows)],
            dst_ref=stage.at[me_t],
            send_sem=s_lat.at[d - 1], recv_sem=r_lat.at[d - 1],
            device_id=((me_t + d) % tiles, me_c), device_id_type=MESH,
        )
        copy.start()
        lat_copies.append(copy)

    zs = chans // 2
    z_copies = []
    for d in (1, zs - 1, 2):
        copy = pltpu.make_async_remote_copy(
            src_ref=we.at[mine], dst_ref=we.at[mine],
            send_sem=s_z.at[d - 1], recv_sem=r_z.at[d - 1],
            device_id=(me_t, ((z + d) % zs) * 2 + core), device_id_type=MESH,
        )
        copy.start()
        z_copies.append((d, copy))
    sib = (me_t, z * 2 + 1 - core)
    sib_copies = []

    def to_sibling(d):
        rows = pl.ds(pl.multiple_of((((z + zs - d) % zs) * 2 + core) * COUT, COUT), COUT)
        copy = pltpu.make_async_remote_copy(
            src_ref=we.at[rows], dst_ref=we.at[rows],
            send_sem=s_sib.at[d], recv_sem=r_sib.at[d],
            device_id=sib, device_id_type=MESH,
        )
        copy.start()
        sib_copies.append(copy)

    to_sibling(0)

    for copy in lat_copies:
        copy.wait_recv()
    own = assign[me_t]
    before = jnp.maximum(own - 1, 0)
    sel[me_c, 0] = stage[own]
    sel[me_c, 1] = stage[before]
    sel_copies = []
    for d in range(1, chans):
        copy = pltpu.make_async_remote_copy(
            src_ref=sel.at[me_c], dst_ref=sel.at[me_c],
            send_sem=s_sel.at[d - 1], recv_sem=r_sel.at[d - 1],
            device_id=(me_t, (me_c + d) % chans), device_id_type=MESH,
        )
        copy.start()
        sel_copies.append(copy)

    for d, copy in z_copies:
        copy.wait_recv()
        to_sibling(d)
    for copy in sel_copies + sib_copies:
        copy.wait_recv()
    for copy in lat_copies + sel_copies + sib_copies + [c for _, c in z_copies]:
        copy.wait_send()


def decode_kernel(
    durations, assign, slot, we, sel, w3, bias, gain, shift,
    out,
    wm, flat, xe, entry, xc, prod, fine, tails, rows, spread, w_sem,
):
    f32, bf16 = jnp.float32, jnp.bfloat16
    w_copies = [
        pltpu.make_async_copy(w3.at[a], wm.at[:, a * CIN:(a + 1) * CIN], w_sem.at[a]) for a in range(3)
    ]
    for copy in w_copies:
        copy.start()

    lane = lax.broadcasted_iota(jnp.int32, (1, CELLS), 1)
    cell_r, cell_q = lane // WT, lane % WT
    diagonal = lax.broadcasted_iota(jnp.int32, (COUT, COUT), 0) == lax.broadcasted_iota(jnp.int32, (COUT, COUT), 1)

    def column(ref):
        return jnp.sum(jnp.where(diagonal, ref[...], 0.0), axis=1, keepdims=True)

    bias_col, gain_col, shift_col = column(bias), column(gain), column(shift)
    own = assign[slot[0]]

    def one_tile(j, tile):
        duration = durations[tile]
        duration_f = duration.astype(f32)
        flat[...] = sel[:, j].astype(f32).reshape(CL * FT, CELLS)
        base = jnp.concatenate([flat[pl.ds(f, CL, stride=FT), :] for f in range(FT)], axis=0)
        for s in range(9):
            b, c = s // 3 - 1, s % 3 - 1
            moved = base
            if s != 4:
                moved = pltpu.roll(base, (-(b * WT + c)) % CELLS, 1)
                inside = (cell_r + b >= 0) & (cell_r + b < CELLS // WT) & (cell_q + c >= 0) & (cell_q + c < WT)
                moved = jnp.where(inside, moved, 0.0)
            moved = moved.astype(bf16)
            for a in range(3):
                for f in range(FT):
                    at = max(f - 2 + a, 0)
                    xe[(9 * a + s) * CL:(9 * a + s + 1) * CL, f * CELLS:(f + 1) * CELLS] = moved[at * CL:(at + 1) * CL]
        last = lax.broadcasted_iota(jnp.int32, (KE - WROWS, FT * CELLS), 0)
        xe[WROWS:, :] = jnp.where(last < 3, 1.0, 0.0).astype(bf16)
        entry[...] = jnp.dot(we[...], xe[...], preferred_element_type=f32)

        frame = lax.broadcasted_iota(jnp.int32, (1, 1, FT * CELLS), 2) // CELLS
        live = (frame < duration).astype(f32)
        members = 1.0 / (GSIZE * CELLS * duration_f)

        def chunk(i, _):
            at = pl.ds(pl.multiple_of(i * COUT, COUT), COUT)
            groups = COUT // GSIZE
            e = entry[at, :].reshape(groups, GSIZE, FT * CELLS)
            mean = jnp.sum(e * live, axis=(1, 2), keepdims=True) * members
            centred = e - mean
            var = jnp.sum(centred * centred * live, axis=(1, 2), keepdims=True) * members
            extra = we[at, KE - CELLS:].astype(f32)
            start = WROWS + 3 - (KE - CELLS)
            g1 = jnp.sum(jnp.where((lane >= start) & (lane < start + 3), extra, 0.0), axis=1, keepdims=True)
            b1 = jnp.sum(jnp.where((lane >= start + 3) & (lane < start + 6), extra, 0.0), axis=1, keepdims=True)
            scale = g1.reshape(groups, GSIZE, 1) * lax.rsqrt(var + EPS)
            half = centred * (0.5 * scale) + 0.5 * b1.reshape(groups, GSIZE, 1)
            coarse = (half * jnp.tanh(half) + half).astype(bf16).reshape(COUT, FT * CELLS)
            for a in range(3):
                to = pl.ds(pl.multiple_of(a * CIN + i * COUT, COUT), COUT)
                skip = 2 - a
                for f in range(skip):
                    xc[to, f * CELLS:(f + 1) * CELLS] = coarse[:, :CELLS]
                xc[to, skip * CELLS:] = coarse[:, :(FT - skip) * CELLS]
            return 0

        lax.fori_loop(0, CIN // COUT, chunk, 0)

        prod[...] = jnp.dot(wm[...], xc[...], preferred_element_type=f32)

        total = jnp.zeros((COUT, CELLS), f32)
        top, bottom = cell_r >= 1, cell_r < CELLS // WT - 1
        left, right = cell_q >= 1, cell_q < WT - 1
        for f in range(FT):
            p = [prod[s * COUT:(s + 1) * COUT, f * CELLS:(f + 1) * CELLS] for s in range(9)]
            p[4] = p[4] + bias_col
            upper, lower = [], []
            for c in range(3):
                upper.append(jnp.where(top, pltpu.roll(p[c], WT, 1), 0.0) + (p[3 + c] + p[6 + c]))
                lower.append((p[c] + p[3 + c]) + jnp.where(bottom, pltpu.roll(p[6 + c], CELLS - WT, 1), 0.0))
            phases = []
            for r in (upper, lower):
                phases.append(jnp.where(left, pltpu.roll(r[0], 1, 1), 0.0) + (r[1] + r[2]))
                phases.append((r[0] + r[1]) + jnp.where(right, pltpu.roll(r[2], CELLS - 1, 1), 0.0))
            for n in range(4):
                fine[f, :, n * CELLS:(n + 1) * CELLS] = phases[n]
            total = total + ((phases[0] + phases[1]) + (phases[2] + phases[3])) * (f < duration).astype(f32)

        members = 1.0 / (GSIZE * 4 * CELLS * duration_f)

        def per_group(x):
            x = jnp.sum(x.reshape(COUT // GSIZE, GSIZE, CELLS), axis=(1, 2), keepdims=True) * members
            return jnp.broadcast_to(x, (COUT // GSIZE, GSIZE, 1)).reshape(COUT, 1)

        mean = per_group(total)
        total = jnp.zeros((COUT, CELLS), f32)
        for f in range(FT):
            sums = jnp.zeros((COUT, CELLS), f32)
            for n in range(4):
                centred = fine[f, :, n * CELLS:(n + 1) * CELLS] - mean
                sums = sums + centred * centred
            total = total + sums * (f < duration).astype(f32)
        scale = 0.5 * gain_col * lax.rsqrt(per_group(total) + EPS)
        offset = 0.5 * shift_col

        def finish(f):
            half = (fine[f] - mean) * scale + offset
            return (half * jnp.tanh(half) + half).astype(bf16)

        return duration, finish

    before = jnp.maximum(own - 1, 0)
    for copy in w_copies:
        copy.wait()
    duration, finish = one_tile(1, before)
    for k in range(OV):
        tails[k] = finish(duration - OV + k)
    duration, finish = one_tile(0, own)
    for f in range(FT):
        result = jnp.where(f < duration, finish(f).astype(f32), 0.0)
        if f < OV:
            w = (f + 1) / (OV + 1)
            blended = result * w + tails[f].astype(f32) * (1.0 - w)
            result = jnp.where(own == 0, result, blended)
        rows[f * COUT:(f + 1) * COUT, :] = result.astype(bf16)

    col = lax.broadcasted_iota(jnp.int32, (1, 4 * CELLS), 1)
    fr, fc = col // (2 * WT), col % (2 * WT)
    source = ((fr % 2) * 2 + fc % 2) * CELLS + (fr // 2) * WT + fc // 2
    permute = (lax.broadcasted_iota(jnp.int32, (4 * CELLS, 4 * CELLS), 0) == source).astype(f32).astype(bf16)
    whole = jnp.dot(rows[...], permute, preferred_element_type=f32)
    for f in range(FT):
        for n in range(4):
            spread[n, pl.ds(f, COUT, stride=FT), :] = whole[f * COUT:(f + 1) * COUT, n * CELLS:(n + 1) * CELLS]
    for n in range(4):
        out[:, :, n * CELLS:(n + 1) * CELLS] = spread[n].astype(bf16).reshape(COUT, FT, CELLS)


def gather(assign, lat, wt, bias, gain, shift, tiles, chans):
    vmem = pl.BlockSpec(memory_space=pltpu.VMEM)
    dma = pltpu.SemaphoreType.DMA
    part = CL // chans
    return pl.pallas_call(
        functools.partial(gather_kernel, tiles, chans),
        out_shape=(
            jax.ShapeDtypeStruct((CIN, KE), jnp.bfloat16),
            jax.ShapeDtypeStruct((chans, 2, part, FT, CELLS), jnp.bfloat16),
        ),
        in_specs=[pl.BlockSpec(memory_space=pltpu.SMEM)] + [vmem] * 5,
        out_specs=(vmem, vmem),
        scratch_shapes=[
            pltpu.VMEM((KE, COUT), jnp.bfloat16),
            pltpu.VMEM((tiles, part, FT, CELLS), jnp.bfloat16),
            dma((tiles - 1,)), dma((tiles - 1,)),
            dma((3,)), dma((3,)),
            dma((4,)), dma((4,)),
            dma((chans - 1,)), dma((chans - 1,)),
        ],
        compiler_params=pltpu.CompilerParams(collective_id=0, has_side_effects=True),
    )(assign, lat, wt, bias, gain, shift)


def decode(durations, assign, slot, we, sel, w3, bias, gain, shift):
    vmem = pl.BlockSpec(memory_space=pltpu.VMEM)
    smem = pl.BlockSpec(memory_space=pltpu.SMEM)
    bf16, f32 = jnp.bfloat16, jnp.float32
    return pl.pallas_call(
        decode_kernel,
        out_shape=jax.ShapeDtypeStruct((COUT, FT, 4 * CELLS), bf16),
        in_specs=[smem, smem, smem, vmem, vmem, pl.BlockSpec(memory_space=pl.ANY), vmem, vmem, vmem],
        out_specs=vmem,
        scratch_shapes=[
            pltpu.VMEM((9 * COUT, 3 * CIN), bf16),
            pltpu.VMEM((CL * FT, CELLS), f32),
            pltpu.VMEM((KE, FT * CELLS), bf16),
            pltpu.VMEM((CIN, FT * CELLS), f32),
            pltpu.VMEM((3 * CIN, FT * CELLS), bf16),
            pltpu.VMEM((9 * COUT, FT * CELLS), f32),
            pltpu.VMEM((FT, COUT, 4 * CELLS), f32),
            pltpu.VMEM((OV, COUT, 4 * CELLS), bf16),
            pltpu.VMEM((FT * COUT, 4 * CELLS), bf16),
            pltpu.VMEM((4, FT * COUT, CELLS), f32),
            pltpu.SemaphoreType.DMA((3,)),
        ],
        compiler_params=pltpu.CompilerParams(vmem_limit_bytes=56 * 1024 * 1024),
    )(durations, assign, slot, we, sel, w3, bias, gain, shift)


def solution(mesh):
    tiles, chans = mesh.shape["tile"], mesh.shape["chan"]

    def local(latents, durations, assignment, entry_weight, entry_bias, first_gain, first_shift,
              mixer_weight, mixer_bias, second_gain, second_shift):
        wt = jnp.transpose(entry_weight, (0, 2, 1)).reshape(WROWS, COUT)
        we, sel = gather(
            assignment, latents[0], wt, entry_bias[None], first_gain[None], first_shift[None], tiles, chans
        )
        slot = lax.axis_index("tile").astype(jnp.int32)[None]
        out = decode(
            durations, assignment, slot, we, sel, mixer_weight.reshape(3, 9 * COUT, CIN),
            mixer_bias[None], second_gain[None], second_shift[None],
        )
        return out[None]

    in_specs = (
        P("tile", None, None, None), P(), P(), P(None, "chan", None), P("chan"), P("chan"), P("chan"),
        P(None, "chan", None), P("chan"), P("chan"), P("chan"),
    )
    return jax.shard_map(
        local, mesh=mesh, in_specs=in_specs, out_specs=P("tile", "chan", None, None), check_vma=False
    )
```

```python
import functools

import jax
import jax.numpy as jnp
from jax import lax
from jax.experimental import pallas as pl
from jax.experimental.pallas import tpu as pltpu
from jax.sharding import PartitionSpec as P

MESH = pl.DeviceIdType.MESH
GSIZE = 16
OV = 3
FT = 8
WT = 16
CELLS = 128
CL = 16
COUT = 64
CIN = 512
KE = 512
WROWS = 432
EARLY = 1
EPS = 1e-06


def three_parts(x):
    hi = x.astype(jnp.bfloat16).astype(jnp.float32)
    rest = x - hi
    mid = rest.astype(jnp.bfloat16).astype(jnp.float32)
    return hi, mid, rest - mid


def gather_kernel(
    tiles, chans, prepare_rest,
    assign, lat, wt, bias, gain, shift,
    we, sel,
    ext, stage,
    s_lat, r_lat, s_z, r_z, s_sib, r_sib, s_sel, r_sel, ready,
):
    me_t = lax.axis_index("tile")
    me_c = lax.axis_index("chan")
    z, core = me_c // 2, me_c % 2
    zs = chans // 2
    sibling = (me_t, z * 2 + 1 - core)

    barrier = pltpu.get_barrier_semaphore()

    @pl.when(core == 0)
    def _():
        for d in range(1, zs):
            pl.semaphore_signal(barrier, inc=1, device_id=(me_t, ((z + d) % zs) * 2), device_id_type=MESH)

    @pl.when(core == 1)
    def _():
        pl.semaphore_signal(barrier, inc=1, device_id=sibling, device_id_type=MESH)
        for d in range(1, tiles):
            pl.semaphore_signal(barrier, inc=1, device_id=((me_t + d) % tiles, me_c), device_id_type=MESH)

    ext[:WROWS, :] = wt[...]
    row = lax.broadcasted_iota(jnp.int32, (16, COUT), 0)
    packed = jnp.zeros((16, COUT), jnp.float32)
    for base, ref in ((0, bias), (3, gain), (6, shift)):
        for at, piece in enumerate(three_parts(ref[...])):
            packed = jnp.where(row == base + at, piece, packed)
    ext[WROWS:WROWS + 16, :] = packed.astype(jnp.bfloat16)
    ext[WROWS + 16:, :] = jnp.zeros((KE - WROWS - 16, COUT), jnp.bfloat16)
    eye = (
        lax.broadcasted_iota(jnp.int32, (COUT, COUT), 0)
        == lax.broadcasted_iota(jnp.int32, (COUT, COUT), 1)
    ).astype(jnp.bfloat16)

    def shard(chip, half):
        return pl.ds(pl.multiple_of((chip * 2 + half) * COUT, COUT), COUT)

    we[shard(z, core), :] = lax.dot_general(
        eye, ext[...], (((1,), (1,)), ((), ())), preferred_element_type=jnp.float32
    ).astype(jnp.bfloat16)

    def lat_copy(d):
        return pltpu.make_async_remote_copy(
            src_ref=lat, dst_ref=stage.at[me_t],
            send_sem=s_lat.at[d - 1], recv_sem=r_lat.at[d - 1],
            device_id=((me_t + d) % tiles, me_c), device_id_type=MESH,
        )

    def z_copy(d, half):
        rows = shard(z, half)
        return pltpu.make_async_remote_copy(
            src_ref=we.at[rows], dst_ref=we.at[rows],
            send_sem=s_z.at[d - 1, half], recv_sem=r_z.at[d - 1, half],
            device_id=(me_t, ((z + d) % zs) * 2), device_id_type=MESH,
        )

    def sib_copy(d, half):
        rows = shard((z + zs - d) % zs, half)
        return pltpu.make_async_remote_copy(
            src_ref=we.at[rows], dst_ref=we.at[rows],
            send_sem=s_sib.at[d, half], recv_sem=r_sib.at[d, half],
            device_id=sibling, device_id_type=MESH,
        )

    sel_copy = pltpu.make_async_remote_copy(
        src_ref=sel, dst_ref=sel, send_sem=s_sel, recv_sem=r_sel, device_id=sibling, device_id_type=MESH,
    )
    order = (1, 2, zs - 1)

    prepare_rest()

    @pl.when(core == 0)
    def _():
        pl.semaphore_wait(barrier, zs)
        pl.semaphore_signal(ready, inc=1, device_id=sibling, device_id_type=MESH)
        for d in order:
            z_copy(d, 0).start()
        sib_copy(0, 0).start()
        sib_copy(0, 1).wait_recv()
        for d in order:
            z_copy(d, 1).start()
        for d in order:
            for half in range(2):
                z_copy(d, half).wait_recv()
                sib_copy(d, half).start()
        sel_copy.wait_recv()
        for d in order:
            for half in range(2):
                z_copy(d, half).wait_send()
                sib_copy(d, half).wait_send()
        sib_copy(0, 0).wait_send()

    @pl.when(core == 1)
    def _():
        def send_weights():
            pl.semaphore_wait(ready, 1)
            sib_copy(0, 1).start()

        def send_latents():
            pl.semaphore_wait(barrier, tiles - 1)
            for d in range(1, tiles):
                lat_copy(d).start()

        @pl.when(z < EARLY)
        def _():
            send_latents()
            send_weights()

        @pl.when(z >= EARLY)
        def _():
            send_weights()
            send_latents()

        stage[me_t] = lat[...]
        for d in range(1, tiles):
            lat_copy(d).wait_recv()
        own = assign[me_t]
        sel[0] = stage[own]
        sel[1] = stage[jnp.maximum(own - 1, 0)]
        sel_copy.start()
        sib_copy(0, 0).wait_recv()
        for d in order:
            for half in range(2):
                sib_copy(d, half).wait_recv()
        for d in range(1, tiles):
            lat_copy(d).wait_send()
        sel_copy.wait_send()
        sib_copy(0, 1).wait_send()


def decode_kernel(
    w_copies, durations, assign, we, sel, bias, gain, shift,
    out, wm, flat, xe, entry, xp, prod, fine, tails, rows, spread, permute,
):
    f32, bf16 = jnp.float32, jnp.bfloat16
    lane = lax.broadcasted_iota(jnp.int32, (1, CELLS), 1)
    cell_r, cell_q = lane // WT, lane % WT
    diagonal = lax.broadcasted_iota(jnp.int32, (COUT, COUT), 0) == lax.broadcasted_iota(jnp.int32, (COUT, COUT), 1)

    def column(ref):
        return jnp.sum(jnp.where(diagonal, ref[...], 0.0), axis=1, keepdims=True)

    bias_col, gain_col, shift_col = column(bias), column(gain), column(shift)
    own = assign[lax.axis_index("tile")]
    duration_of = (durations[own], durations[jnp.maximum(own - 1, 0)])
    groups = COUT // GSIZE

    def frame(f):
        return slice(f * CELLS, (f + 1) * CELLS)

    def add_live(terms, duration):
        total = terms[0]
        for f in range(1, FT):
            total = total + (terms[f] if f < FT // 2 else terms[f] * (f < duration).astype(f32))
        return total

    for j in range(2):
        flat[...] = sel[j].astype(f32).reshape(CL * FT, CELLS)
        base = jnp.concatenate([flat[pl.ds(f, CL, stride=FT), :] for f in range(FT)], axis=0)
        for s in range(9):
            b, c = s // 3 - 1, s % 3 - 1
            moved = base
            if s != 4:
                moved = pltpu.roll(base, (-(b * WT + c)) % CELLS, 1)
                inside = (cell_r + b >= 0) & (cell_r + b < CELLS // WT) & (cell_q + c >= 0) & (cell_q + c < WT)
                moved = jnp.where(inside, moved, 0.0)
            moved = moved.astype(bf16)
            for a in range(3):
                for f in range(FT):
                    at = max(f - 2 + a, 0)
                    xe[j, (9 * a + s) * CL:(9 * a + s + 1) * CL, frame(f)] = moved[at * CL:(at + 1) * CL]
        entry[j] = jnp.dot(we[...], xe[j], preferred_element_type=f32)

    chunks = [slice(i * COUT, (i + 1) * COUT) for i in range(CIN // COUT)]

    def group_sum(x, members):
        return jnp.sum(x.reshape(groups, GSIZE, CELLS), axis=(1, 2), keepdims=True) * members

    def spread_rows(x):
        return jnp.broadcast_to(x, (groups, GSIZE, 1)).reshape(COUT, 1)

    means, scales = {}, {}
    members = [1.0 / (GSIZE * CELLS * d.astype(f32)) for d in duration_of]
    for j in range(2):
        for i, at in enumerate(chunks):
            total = add_live([entry[j, at, frame(f)] for f in range(FT)], duration_of[j])
            means[j, i] = spread_rows(group_sum(total, members[j]))
    for j in range(2):
        for i, at in enumerate(chunks):
            squares = []
            for f in range(FT):
                centred = entry[j, at, frame(f)] - means[j, i]
                squares.append(centred * centred)
            var = group_sum(add_live(squares, duration_of[j]), members[j])
            scales[j, i] = spread_rows(0.5 * lax.rsqrt(var + EPS))
    start = WROWS + 3 - (KE - CELLS)
    for i, at in enumerate(chunks):
        extra = we[at, KE - CELLS:].astype(f32)
        g1 = jnp.sum(jnp.where((lane >= start) & (lane < start + 3), extra, 0.0), axis=1, keepdims=True)
        b1 = jnp.sum(jnp.where((lane >= start + 3) & (lane < start + 6), extra, 0.0), axis=1, keepdims=True)
        for j in range(2):
            scale = scales[j, i] * g1
            offset = 0.5 * b1 - means[j, i] * scale
            for f in range(FT):
                half = entry[j, at, frame(f)] * scale + offset
                coarse = (half * jnp.tanh(half) + half).astype(bf16)
                xp[j, at, frame(f + 2)] = coarse
                if f == 0:
                    xp[j, at, frame(0)] = coarse
                    xp[j, at, frame(1)] = coarse

    for copy in w_copies:
        copy.wait()
    top, bottom = cell_r >= 1, cell_r < CELLS // WT - 1
    left, right = cell_q >= 1, cell_q < WT - 1

    def mix(j):
        delayed = jnp.concatenate([xp[j, :, a * CELLS:(a + FT) * CELLS] for a in range(3)], axis=0)
        prod[j] = jnp.dot(wm[...], delayed, preferred_element_type=f32)

    def upsampled(j):
        sums = []
        for f in range(FT):
            p = [prod[j, s * COUT:(s + 1) * COUT, frame(f)] for s in range(9)]
            p[4] = p[4] + bias_col
            upper, lower = [], []
            for c in range(3):
                upper.append(jnp.where(top, pltpu.roll(p[c], WT, 1), 0.0) + (p[3 + c] + p[6 + c]))
                lower.append((p[c] + p[3 + c]) + jnp.where(bottom, pltpu.roll(p[6 + c], CELLS - WT, 1), 0.0))
            phases = []
            for r in (upper, lower):
                phases.append(jnp.where(left, pltpu.roll(r[0], 1, 1), 0.0) + (r[1] + r[2]))
                phases.append((r[0] + r[1]) + jnp.where(right, pltpu.roll(r[2], CELLS - 1, 1), 0.0))
            for n in range(4):
                fine[j, f, :, frame(n)] = phases[n]
            sums.append((phases[0] + phases[1]) + (phases[2] + phases[3]))
        members = 1.0 / (GSIZE * 4 * CELLS * duration_of[j].astype(f32))
        mean = spread_rows(group_sum(add_live(sums, duration_of[j]), members))
        sums = []
        for f in range(FT):
            total = None
            for n in range(4):
                centred = fine[j, f, :, frame(n)] - mean
                total = centred * centred if total is None else total + centred * centred
            sums.append(total)
        var = group_sum(add_live(sums, duration_of[j]), members)
        scale = gain_col * spread_rows(0.5 * lax.rsqrt(var + EPS))
        offset = 0.5 * shift_col - mean * scale

        def finish(f):
            half = fine[j, f] * scale + offset
            return (half * jnp.tanh(half) + half).astype(bf16)

        return finish

    mix(1)
    finish = upsampled(1)
    for k in range(OV):
        tails[k] = finish(jnp.clip(duration_of[1] - OV + k, 0, FT - 1))
    mix(0)
    finish = upsampled(0)
    for f in range(FT):
        result = finish(f).astype(f32)
        if f >= FT // 2:
            result = jnp.where(f < duration_of[0], result, 0.0)
        if f < OV:
            w = (f + 1) / (OV + 1)
            blended = result * w + tails[f].astype(f32) * (1.0 - w)
            result = jnp.where(own == 0, result, blended)
        rows[f * COUT:(f + 1) * COUT, :] = result.astype(bf16)

    whole = jnp.dot(rows[...], permute[...], preferred_element_type=f32)
    for f in range(FT):
        for n in range(4):
            spread[n, pl.ds(f, COUT, stride=FT), :] = whole[f * COUT:(f + 1) * COUT, frame(n)]
    for n in range(4):
        out[:, :, frame(n)] = spread[n].astype(bf16).reshape(COUT, FT, CELLS)


def prepare(xe, permute):
    last = lax.broadcasted_iota(jnp.int32, (KE - WROWS, FT * CELLS), 0)
    ones = jnp.where(last < 3, 1.0, 0.0).astype(jnp.bfloat16)
    for j in range(2):
        xe[j, WROWS:, :] = ones
    col = lax.broadcasted_iota(jnp.int32, (1, 4 * CELLS), 1)
    fr, fc = col // (2 * WT), col % (2 * WT)
    source = ((fr % 2) * 2 + fc % 2) * CELLS + (fr // 2) * WT + fc // 2
    found = lax.broadcasted_iota(jnp.int32, (4 * CELLS, 4 * CELLS), 0) == source
    permute[...] = found.astype(jnp.float32).astype(jnp.bfloat16)


def fused_kernel(
    tiles, chans,
    durations, assign, lat, wt, bias1, gain1, shift1, w3, bias2, gain2, shift2,
    out,
    we, sel, ext, stage,
    wm, flat, xe, entry, xp, prod, fine, tails, rows, spread, permute,
    s_lat, r_lat, s_z, r_z, s_sib, r_sib, s_sel, r_sel, ready, w_sem,
):
    w_copies = [
        pltpu.make_async_copy(w3.at[a], wm.at[:, a * CIN:(a + 1) * CIN], w_sem.at[a]) for a in range(3)
    ]
    for copy in w_copies:
        copy.start()
    gather_kernel(
        tiles, chans, lambda: prepare(xe, permute), assign, lat, wt, bias1, gain1, shift1, we, sel, ext, stage,
        s_lat, r_lat, s_z, r_z, s_sib, r_sib, s_sel, r_sel, ready,
    )
    decode_kernel(
        w_copies, durations, assign, we, sel, bias2, gain2, shift2,
        out, wm, flat, xe, entry, xp, prod, fine, tails, rows, spread, permute,
    )


def fused(tiles, chans, *args):
    vmem = pl.BlockSpec(memory_space=pltpu.VMEM)
    smem = pl.BlockSpec(memory_space=pltpu.SMEM)
    hbm = pl.BlockSpec(memory_space=pl.ANY)
    dma = pltpu.SemaphoreType.DMA
    bf16, f32 = jnp.bfloat16, jnp.float32
    return pl.pallas_call(
        functools.partial(fused_kernel, tiles, chans),
        out_shape=jax.ShapeDtypeStruct((COUT, FT, 4 * CELLS), bf16),
        in_specs=[smem, smem] + [vmem] * 5 + [hbm] + [vmem] * 3,
        out_specs=vmem,
        scratch_shapes=[
            pltpu.VMEM((CIN, KE), bf16),
            pltpu.VMEM((2, CL, FT, CELLS), bf16),
            pltpu.VMEM((KE, COUT), bf16),
            pltpu.VMEM((tiles, CL, FT, CELLS), bf16),
            pltpu.VMEM((9 * COUT, 3 * CIN), bf16),
            pltpu.VMEM((CL * FT, CELLS), f32),
            pltpu.VMEM((2, KE, FT * CELLS), bf16),
            pltpu.VMEM((2, CIN, FT * CELLS), f32),
            pltpu.VMEM((2, CIN, (FT + 2) * CELLS), bf16),
            pltpu.VMEM((2, 9 * COUT, FT * CELLS), f32),
            pltpu.VMEM((2, FT, COUT, 4 * CELLS), f32),
            pltpu.VMEM((OV, COUT, 4 * CELLS), bf16),
            pltpu.VMEM((FT * COUT, 4 * CELLS), bf16),
            pltpu.VMEM((4, FT * COUT, CELLS), f32),
            pltpu.VMEM((4 * CELLS, 4 * CELLS), bf16),
            dma((tiles - 1,)), dma((tiles - 1,)),
            dma((3, 2)), dma((3, 2)),
            dma((4, 2)), dma((4, 2)),
            dma, dma, pltpu.SemaphoreType.REGULAR,
            dma((3,)),
        ],
        compiler_params=pltpu.CompilerParams(
            collective_id=0, has_side_effects=True, vmem_limit_bytes=56 * 1024 * 1024
        ),
    )(*args)


def solution(mesh):
    tiles, chans = mesh.shape["tile"], mesh.shape["chan"]

    def local(latents, durations, assignment, entry_weight, entry_bias, first_gain, first_shift,
              mixer_weight, mixer_bias, second_gain, second_shift):
        wt = jnp.transpose(entry_weight, (0, 2, 1)).reshape(WROWS, COUT)
        out = fused(
            tiles, chans, durations, assignment, latents[0], wt, entry_bias[None], first_gain[None],
            first_shift[None], mixer_weight.reshape(3, 9 * COUT, CIN), mixer_bias[None], second_gain[None],
            second_shift[None],
        )
        return out[None]

    in_specs = (
        P("tile", None, None, None), P(), P(), P(None, "chan", None), P("chan"), P("chan"), P("chan"),
        P(None, "chan", None), P("chan"), P("chan"), P("chan"),
    )
    return jax.shard_map(
        local, mesh=mesh, in_specs=in_specs, out_specs=P("tile", "chan", None, None), check_vma=False
    )
```

```python
import functools

import jax
import jax.numpy as jnp
from jax import lax
from jax.experimental import pallas as pl
from jax.experimental.pallas import tpu as pltpu
from jax.sharding import PartitionSpec as P

MESH = pl.DeviceIdType.MESH
GSIZE = 16
OV = 3
FT = 8
WT = 16
CELLS = 128
CL = 16
COUT = 64
CIN = 512
KE = 512
WROWS = 432
EARLY = 1
EPS = 1e-06


def three_parts(x):
    hi = x.astype(jnp.bfloat16).astype(jnp.float32)
    rest = x - hi
    mid = rest.astype(jnp.bfloat16).astype(jnp.float32)
    return hi, mid, rest - mid


def gather_kernel(
    tiles, chans, prepare_rest, start_loads, loads, own_copy,
    assign, lat, params,
    we, sel,
    ext, stage,
    s_lat, r_lat, s_z, r_z, s_sib, r_sib, s_sel, r_sel, ready,
):
    me_t = lax.axis_index("tile")
    me_c = lax.axis_index("chan")
    z, core = me_c // 2, me_c % 2
    zs = chans // 2
    sibling = (me_t, z * 2 + 1 - core)

    barrier = pltpu.get_barrier_semaphore()

    @pl.when(core == 0)
    def _():
        for d in range(1, zs):
            pl.semaphore_signal(barrier, inc=1, device_id=(me_t, ((z + d) % zs) * 2), device_id_type=MESH)

    @pl.when(core == 1)
    def _():
        pl.semaphore_signal(barrier, inc=1, device_id=sibling, device_id_type=MESH)
        for d in range(1, tiles):
            pl.semaphore_signal(barrier, inc=1, device_id=((me_t + d) % tiles, me_c), device_id_type=MESH)

    start_loads()
    for copy in loads:
        copy.wait()
    row = lax.broadcasted_iota(jnp.int32, (16, COUT), 0)
    packed = jnp.zeros((16, COUT), jnp.float32)
    for n in range(3):
        for at, piece in enumerate(three_parts(params[n])):
            packed = jnp.where(row == 3 * n + at, piece, packed)
    ext[WROWS:WROWS + 16, :] = packed.astype(jnp.bfloat16)
    ext[WROWS + 16:, :] = jnp.zeros((KE - WROWS - 16, COUT), jnp.bfloat16)
    eye = (
        lax.broadcasted_iota(jnp.int32, (COUT, COUT), 0)
        == lax.broadcasted_iota(jnp.int32, (COUT, COUT), 1)
    ).astype(jnp.bfloat16)

    def shard(chip, half):
        return pl.ds(pl.multiple_of((chip * 2 + half) * COUT, COUT), COUT)

    we[shard(z, core), :] = lax.dot_general(
        eye, ext[...], (((1,), (1,)), ((), ())), preferred_element_type=jnp.float32
    ).astype(jnp.bfloat16)

    def lat_copy(d):
        return pltpu.make_async_remote_copy(
            src_ref=lat, dst_ref=stage.at[me_t],
            send_sem=s_lat.at[d - 1], recv_sem=r_lat.at[d - 1],
            device_id=((me_t + d) % tiles, me_c), device_id_type=MESH,
        )

    def z_copy(d, half):
        rows = shard(z, half)
        return pltpu.make_async_remote_copy(
            src_ref=we.at[rows], dst_ref=we.at[rows],
            send_sem=s_z.at[d - 1, half], recv_sem=r_z.at[d - 1, half],
            device_id=(me_t, ((z + d) % zs) * 2), device_id_type=MESH,
        )

    def sib_copy(d, half):
        rows = shard((z + zs - d) % zs, half)
        return pltpu.make_async_remote_copy(
            src_ref=we.at[rows], dst_ref=we.at[rows],
            send_sem=s_sib.at[d, half], recv_sem=r_sib.at[d, half],
            device_id=sibling, device_id_type=MESH,
        )

    sel_copy = pltpu.make_async_remote_copy(
        src_ref=sel, dst_ref=sel, send_sem=s_sel, recv_sem=r_sel, device_id=sibling, device_id_type=MESH,
    )
    order = (1, 2, zs - 1)

    prepare_rest()

    @pl.when(core == 0)
    def _():
        pl.semaphore_wait(barrier, zs)
        pl.semaphore_signal(ready, inc=1, device_id=sibling, device_id_type=MESH)
        for d in order:
            z_copy(d, 0).start()
        sib_copy(0, 0).start()
        sib_copy(0, 1).wait_recv()
        for d in order:
            z_copy(d, 1).start()
        for d in order:
            for half in range(2):
                z_copy(d, half).wait_recv()
                sib_copy(d, half).start()
        sel_copy.wait_recv()
        for d in order:
            for half in range(2):
                z_copy(d, half).wait_send()
                sib_copy(d, half).wait_send()
        sib_copy(0, 0).wait_send()

    @pl.when(core == 1)
    def _():
        own_copy.start()

        def send_weights():
            pl.semaphore_wait(ready, 1)
            sib_copy(0, 1).start()

        def send_latents():
            pl.semaphore_wait(barrier, tiles - 1)
            for d in range(1, tiles):
                lat_copy(d).start()

        @pl.when(z < EARLY)
        def _():
            send_latents()
            send_weights()

        @pl.when(z >= EARLY)
        def _():
            send_weights()
            send_latents()

        own_copy.wait()
        for d in range(1, tiles):
            lat_copy(d).wait_recv()
        own = assign[me_t]
        sel[0] = stage[own]
        sel[1] = stage[jnp.maximum(own - 1, 0)]
        sel_copy.start()
        sib_copy(0, 0).wait_recv()
        for d in order:
            for half in range(2):
                sib_copy(d, half).wait_recv()
        for d in range(1, tiles):
            lat_copy(d).wait_send()
        sel_copy.wait_send()
        sib_copy(0, 1).wait_send()


def decode_kernel(
    w_copies, durations, assign, we, sel, params,
    out, wm, flat, xe, entry, xp, prod, fine, tails, rows, spread, permute,
):
    f32, bf16 = jnp.float32, jnp.bfloat16
    lane = lax.broadcasted_iota(jnp.int32, (1, CELLS), 1)
    cell_r, cell_q = lane // WT, lane % WT
    diagonal = lax.broadcasted_iota(jnp.int32, (COUT, COUT), 0) == lax.broadcasted_iota(jnp.int32, (COUT, COUT), 1)

    def column(ref):
        return jnp.sum(jnp.where(diagonal, ref, 0.0), axis=1, keepdims=True)

    bias_col, gain_col, shift_col = (column(params[n]) for n in range(3, 6))
    own = assign[lax.axis_index("tile")]
    duration_of = (durations[own], durations[jnp.maximum(own - 1, 0)])
    groups = COUT // GSIZE

    def frame(f):
        return slice(f * CELLS, (f + 1) * CELLS)

    def add_live(terms, duration):
        total = terms[0]
        for f in range(1, FT):
            total = total + (terms[f] if f < FT // 2 else terms[f] * (f < duration).astype(f32))
        return total

    for j in range(2):
        flat[...] = sel[j].astype(f32).reshape(CL * FT, CELLS)
        base = jnp.concatenate([flat[pl.ds(f, CL, stride=FT), :] for f in range(FT)], axis=0)
        for s in range(9):
            b, c = s // 3 - 1, s % 3 - 1
            moved = base
            if s != 4:
                moved = pltpu.roll(base, (-(b * WT + c)) % CELLS, 1)
                inside = (cell_r + b >= 0) & (cell_r + b < CELLS // WT) & (cell_q + c >= 0) & (cell_q + c < WT)
                moved = jnp.where(inside, moved, 0.0)
            moved = moved.astype(bf16)
            for a in range(3):
                for f in range(FT):
                    at = max(f - 2 + a, 0)
                    xe[j, (9 * a + s) * CL:(9 * a + s + 1) * CL, frame(f)] = moved[at * CL:(at + 1) * CL]
        entry[j] = jnp.dot(we[...], xe[j], preferred_element_type=f32)

    chunks = [slice(i * COUT, (i + 1) * COUT) for i in range(CIN // COUT)]

    def group_sum(x, members):
        return jnp.sum(x.reshape(groups, GSIZE, CELLS), axis=(1, 2), keepdims=True) * members

    def spread_rows(x):
        return jnp.broadcast_to(x, (groups, GSIZE, 1)).reshape(COUT, 1)

    means, scales = {}, {}
    members = [1.0 / (GSIZE * CELLS * d.astype(f32)) for d in duration_of]
    for j in range(2):
        for i, at in enumerate(chunks):
            total = add_live([entry[j, at, frame(f)] for f in range(FT)], duration_of[j])
            means[j, i] = spread_rows(group_sum(total, members[j]))
    for j in range(2):
        for i, at in enumerate(chunks):
            squares = []
            for f in range(FT):
                centred = entry[j, at, frame(f)] - means[j, i]
                squares.append(centred * centred)
            var = group_sum(add_live(squares, duration_of[j]), members[j])
            scales[j, i] = spread_rows(0.5 * lax.rsqrt(var + EPS))
    start = WROWS + 3 - (KE - CELLS)
    for i, at in enumerate(chunks):
        extra = we[at, KE - CELLS:].astype(f32)
        g1 = jnp.sum(jnp.where((lane >= start) & (lane < start + 3), extra, 0.0), axis=1, keepdims=True)
        b1 = jnp.sum(jnp.where((lane >= start + 3) & (lane < start + 6), extra, 0.0), axis=1, keepdims=True)
        for j in range(2):
            scale = scales[j, i] * g1
            offset = 0.5 * b1 - means[j, i] * scale
            for f in range(FT):
                half = entry[j, at, frame(f)] * scale + offset
                coarse = (half * jnp.tanh(half) + half).astype(bf16)
                xp[j, at, frame(f + 2)] = coarse
                if f == 0:
                    xp[j, at, frame(0)] = coarse
                    xp[j, at, frame(1)] = coarse

    for copy in w_copies:
        copy.wait()
    top, bottom = cell_r >= 1, cell_r < CELLS // WT - 1
    left, right = cell_q >= 1, cell_q < WT - 1

    def mix(j):
        delayed = jnp.concatenate([xp[j, :, a * CELLS:(a + FT) * CELLS] for a in range(3)], axis=0)
        prod[j] = jnp.dot(wm[...], delayed, preferred_element_type=f32)

    def upsampled(j):
        sums = []
        for f in range(FT):
            p = [prod[j, s * COUT:(s + 1) * COUT, frame(f)] for s in range(9)]
            p[4] = p[4] + bias_col
            upper, lower = [], []
            for c in range(3):
                upper.append(jnp.where(top, pltpu.roll(p[c], WT, 1), 0.0) + (p[3 + c] + p[6 + c]))
                lower.append((p[c] + p[3 + c]) + jnp.where(bottom, pltpu.roll(p[6 + c], CELLS - WT, 1), 0.0))
            phases = []
            for r in (upper, lower):
                phases.append(jnp.where(left, pltpu.roll(r[0], 1, 1), 0.0) + (r[1] + r[2]))
                phases.append((r[0] + r[1]) + jnp.where(right, pltpu.roll(r[2], CELLS - 1, 1), 0.0))
            for n in range(4):
                fine[j, f, :, frame(n)] = phases[n]
            sums.append((phases[0] + phases[1]) + (phases[2] + phases[3]))
        members = 1.0 / (GSIZE * 4 * CELLS * duration_of[j].astype(f32))
        mean = spread_rows(group_sum(add_live(sums, duration_of[j]), members))
        sums = []
        for f in range(FT):
            total = None
            for n in range(4):
                centred = fine[j, f, :, frame(n)] - mean
                total = centred * centred if total is None else total + centred * centred
            sums.append(total)
        var = group_sum(add_live(sums, duration_of[j]), members)
        scale = gain_col * spread_rows(0.5 * lax.rsqrt(var + EPS))
        offset = 0.5 * shift_col - mean * scale

        def finish(f):
            half = fine[j, f] * scale + offset
            return (half * jnp.tanh(half) + half).astype(bf16)

        return finish

    mix(1)
    finish = upsampled(1)
    for k in range(OV):
        tails[k] = finish(jnp.clip(duration_of[1] - OV + k, 0, FT - 1))
    mix(0)
    finish = upsampled(0)
    for f in range(FT):
        result = finish(f).astype(f32)
        if f >= FT // 2:
            result = jnp.where(f < duration_of[0], result, 0.0)
        if f < OV:
            w = (f + 1) / (OV + 1)
            blended = result * w + tails[f].astype(f32) * (1.0 - w)
            result = jnp.where(own == 0, result, blended)
        rows[f * COUT:(f + 1) * COUT, :] = result.astype(bf16)

    whole = jnp.dot(rows[...], permute[...], preferred_element_type=f32)
    for f in range(FT):
        for n in range(4):
            spread[n, pl.ds(f, COUT, stride=FT), :] = whole[f * COUT:(f + 1) * COUT, frame(n)]
    for n in range(4):
        out[:, :, frame(n)] = spread[n].astype(bf16).reshape(COUT, FT, CELLS)


def prepare(xe, permute):
    last = lax.broadcasted_iota(jnp.int32, (KE - WROWS, FT * CELLS), 0)
    ones = jnp.where(last < 3, 1.0, 0.0).astype(jnp.bfloat16)
    for j in range(2):
        xe[j, WROWS:, :] = ones
    col = lax.broadcasted_iota(jnp.int32, (1, 4 * CELLS), 1)
    fr, fc = col // (2 * WT), col % (2 * WT)
    source = ((fr % 2) * 2 + fc % 2) * CELLS + (fr // 2) * WT + fc // 2
    found = lax.broadcasted_iota(jnp.int32, (4 * CELLS, 4 * CELLS), 0) == source
    permute[...] = found.astype(jnp.float32).astype(jnp.bfloat16)


def fused_kernel(
    tiles, chans,
    durations_in, assign_in, lat, wt, bias1, gain1, shift1, w3, bias2, gain2, shift2,
    out,
    durations, assign, params, we, sel, ext, stage,
    wm, flat, xe, entry, xp, prod, fine, tails, rows, spread, permute,
    s_lat, r_lat, s_z, r_z, s_sib, r_sib, s_sel, r_sel, ready, w_sem, load_sem,
):
    me_t = lax.axis_index("tile")
    loads = [pltpu.make_async_copy(wt, ext.at[:WROWS], load_sem.at[0])]
    for n, ref in enumerate((bias1, gain1, shift1, bias2, gain2, shift2)):
        loads.append(pltpu.make_async_copy(ref, params.at[n], load_sem.at[n + 1]))
    loads.append(pltpu.make_async_copy(durations_in, durations, load_sem.at[7]))
    loads.append(pltpu.make_async_copy(assign_in, assign, load_sem.at[8]))
    own_copy = pltpu.make_async_copy(lat, stage.at[me_t], load_sem.at[9])
    w_copies = [
        pltpu.make_async_copy(w3.at[a], wm.at[:, a * CIN:(a + 1) * CIN], w_sem.at[a]) for a in range(3)
    ]

    def start_loads():
        for copy in loads + w_copies:
            copy.start()

    gather_kernel(
        tiles, chans, lambda: prepare(xe, permute), start_loads, loads, own_copy, assign, lat, params, we, sel, ext, stage,
        s_lat, r_lat, s_z, r_z, s_sib, r_sib, s_sel, r_sel, ready,
    )
    decode_kernel(
        w_copies, durations, assign, we, sel, params,
        out, wm, flat, xe, entry, xp, prod, fine, tails, rows, spread, permute,
    )


def fused(tiles, chans, *args):
    vmem = pl.BlockSpec(memory_space=pltpu.VMEM)
    hbm = pl.BlockSpec(memory_space=pl.ANY)
    dma = pltpu.SemaphoreType.DMA
    bf16, f32 = jnp.bfloat16, jnp.float32
    return pl.pallas_call(
        functools.partial(fused_kernel, tiles, chans),
        out_shape=pltpu.VMEM((COUT, FT, 4 * CELLS), bf16),
        in_specs=[hbm] * 11,
        out_specs=vmem,
        scratch_shapes=[
            pltpu.SMEM((tiles,), jnp.int32),
            pltpu.SMEM((tiles,), jnp.int32),
            pltpu.VMEM((6, 1, COUT), f32),
            pltpu.VMEM((CIN, KE), bf16),
            pltpu.VMEM((2, CL, FT, CELLS), bf16),
            pltpu.VMEM((KE, COUT), bf16),
            pltpu.VMEM((tiles, CL, FT, CELLS), bf16),
            pltpu.VMEM((9 * COUT, 3 * CIN), bf16),
            pltpu.VMEM((CL * FT, CELLS), f32),
            pltpu.VMEM((2, KE, FT * CELLS), bf16),
            pltpu.VMEM((2, CIN, FT * CELLS), f32),
            pltpu.VMEM((2, CIN, (FT + 2) * CELLS), bf16),
            pltpu.VMEM((2, 9 * COUT, FT * CELLS), f32),
            pltpu.VMEM((2, FT, COUT, 4 * CELLS), f32),
            pltpu.VMEM((OV, COUT, 4 * CELLS), bf16),
            pltpu.VMEM((FT * COUT, 4 * CELLS), bf16),
            pltpu.VMEM((4, FT * COUT, CELLS), f32),
            pltpu.VMEM((4 * CELLS, 4 * CELLS), bf16),
            dma((tiles - 1,)), dma((tiles - 1,)),
            dma((3, 2)), dma((3, 2)),
            dma((4, 2)), dma((4, 2)),
            dma, dma, pltpu.SemaphoreType.REGULAR,
            dma((3,)),
            dma((10,)),
        ],
        compiler_params=pltpu.CompilerParams(
            collective_id=0, has_side_effects=True, vmem_limit_bytes=56 * 1024 * 1024
        ),
    )(*args)


def solution(mesh):
    tiles, chans = mesh.shape["tile"], mesh.shape["chan"]

    def local(latents, durations, assignment, entry_weight, entry_bias, first_gain, first_shift,
              mixer_weight, mixer_bias, second_gain, second_shift):
        wt = jnp.transpose(entry_weight, (0, 2, 1)).reshape(WROWS, COUT)
        out = fused(
            tiles, chans, durations, assignment, latents[0], wt, entry_bias[None], first_gain[None],
            first_shift[None], mixer_weight.reshape(3, 9 * COUT, CIN), mixer_bias[None], second_gain[None],
            second_shift[None],
        )
        return out[None]

    in_specs = (
        P("tile", None, None, None), P(), P(), P(None, "chan", None), P("chan"), P("chan"), P("chan"),
        P(None, "chan", None), P("chan"), P("chan"), P("chan"),
    )
    return jax.shard_map(
        local, mesh=mesh, in_specs=in_specs, out_specs=P("tile", "chan", None, None), check_vma=False
    )
```

```python
import functools

import jax
import jax.numpy as jnp
from jax import lax
from jax.experimental import pallas as pl
from jax.experimental.pallas import tpu as pltpu
from jax.sharding import PartitionSpec as P

MESH = pl.DeviceIdType.MESH
GSIZE = 16
OV = 3
FT = 8
WT = 16
CELLS = 128
CL = 16
COUT = 64
CIN = 512
KE = 512
WROWS = 432
EARLY = 1
LATE = 2
EPS = 1e-06


def three_parts(x):
    hi = x.astype(jnp.bfloat16).astype(jnp.float32)
    rest = x - hi
    mid = rest.astype(jnp.bfloat16).astype(jnp.float32)
    return hi, mid, rest - mid


def gather_kernel(
    tiles, chans, prepare_rest, start_loads, loads, own_copy,
    assign, lat, params,
    we, sel,
    ext, stage,
    s_lat, r_lat, s_z, r_z, s_sib, r_sib, s_sel, r_sel, ready,
):
    me_t = lax.axis_index("tile")
    me_c = lax.axis_index("chan")
    z, core = me_c // 2, me_c % 2
    zs = chans // 2
    sibling = (me_t, z * 2 + 1 - core)

    barrier = pltpu.get_barrier_semaphore()

    @pl.when(core == 0)
    def _():
        for d in range(1, zs):
            pl.semaphore_signal(barrier, inc=1, device_id=(me_t, ((z + d) % zs) * 2), device_id_type=MESH)

    @pl.when(core == 1)
    def _():
        for d in range(zs):
            pl.semaphore_signal(barrier, inc=1, device_id=(me_t, ((z + d) % zs) * 2), device_id_type=MESH)
        for d in range(1, tiles):
            pl.semaphore_signal(barrier, inc=1, device_id=((me_t + d) % tiles, me_c), device_id_type=MESH)

    start_loads()

    def shard(chip, half):
        return pl.ds(pl.multiple_of((chip * 2 + half) * COUT, COUT), COUT)

    def pack_weights():
        for copy in loads:
            copy.wait()
        row = lax.broadcasted_iota(jnp.int32, (16, COUT), 0)
        packed = jnp.zeros((16, COUT), jnp.float32)
        for n in range(3):
            for at, piece in enumerate(three_parts(params[n])):
                packed = jnp.where(row == 3 * n + at, piece, packed)
        ext[WROWS:WROWS + 16, :] = packed.astype(jnp.bfloat16)
        ext[WROWS + 16:, :] = jnp.zeros((KE - WROWS - 16, COUT), jnp.bfloat16)
        eye = (
            lax.broadcasted_iota(jnp.int32, (COUT, COUT), 0)
            == lax.broadcasted_iota(jnp.int32, (COUT, COUT), 1)
        ).astype(jnp.bfloat16)

        we[shard(z, core), :] = lax.dot_general(
            eye, ext[...], (((1,), (1,)), ((), ())), preferred_element_type=jnp.float32
        ).astype(jnp.bfloat16)

    reach = sorted(range(1, tiles), key=lambda d: -(min(d // 4, 4 - d // 4) + min(d % 4, 4 - d % 4)))

    def lat_peer(d):
        y = (me_t // 4 + d // 4) % 4
        return y * 4 + (me_t + d) % 4

    def lat_copy(d):
        return pltpu.make_async_remote_copy(
            src_ref=lat, dst_ref=stage.at[me_t],
            send_sem=s_lat.at[d - 1], recv_sem=r_lat.at[d - 1],
            device_id=(lat_peer(d), me_c), device_id_type=MESH,
        )

    def z_copy(d):
        rows = shard(z, core)
        return pltpu.make_async_remote_copy(
            src_ref=we.at[rows], dst_ref=we.at[rows],
            send_sem=s_z.at[d - 1], recv_sem=r_z.at[d - 1],
            device_id=(me_t, ((z + d) % zs) * 2 + core), device_id_type=MESH,
        )

    def sib_copy(d):
        rows = shard((z + zs - d) % zs, core)
        return pltpu.make_async_remote_copy(
            src_ref=we.at[rows], dst_ref=we.at[rows],
            send_sem=s_sib.at[d], recv_sem=r_sib.at[d],
            device_id=sibling, device_id_type=MESH,
        )

    def send_own():
        for d in order:
            z_copy(d).start()
        sib_copy(0).start()

    def hand_on():
        for d in order:
            z_copy(d).wait_recv()
            sib_copy(d).start()

    def finish_weights():
        for d in range(zs):
            sib_copy(d).wait_recv()

    sel_copy = pltpu.make_async_remote_copy(
        src_ref=sel, dst_ref=sel, send_sem=s_sel, recv_sem=r_sel, device_id=sibling, device_id_type=MESH,
    )
    order = (2, 1, zs - 1)

    @pl.when(core == 0)
    def _():
        def meet():
            pl.semaphore_wait(barrier, chans - 1)
            pl.semaphore_signal(ready, inc=1, device_id=sibling, device_id_type=MESH)

        @pl.when(z < LATE)
        def _():
            pack_weights()
            meet()

        @pl.when(z >= LATE)
        def _():
            meet()
            pack_weights()

        send_own()
        prepare_rest()
        hand_on()
        finish_weights()
        sel_copy.wait_recv()

    @pl.when(core == 1)
    def _():
        own_copy.start()

        def send_weights():
            pl.semaphore_wait(ready, 1)
            send_own()

        def send_latents():
            pl.semaphore_wait(barrier, tiles - 1)
            for d in reach:
                lat_copy(d).start()

        first = (z < EARLY) | ((z == EARLY) & (me_t % 4 > 0) & (me_t > 3))

        @pl.when(first)
        def _():
            send_latents()
            pack_weights()
            send_weights()

        @pl.when(jnp.logical_not(first))
        def _():
            pack_weights()
            send_weights()
            send_latents()

        prepare_rest()
        own_copy.wait()
        for d in range(1, tiles):
            lat_copy(d).wait_recv()
        own = assign[me_t]
        sel[0] = stage[own]
        sel[1] = stage[jnp.maximum(own - 1, 0)]
        sel_copy.start()
        hand_on()
        finish_weights()

    def drain():
        for d in order:
            z_copy(d).wait_send()
        for d in range(zs):
            sib_copy(d).wait_send()

        @pl.when(core == 1)
        def _():
            for d in range(1, tiles):
                lat_copy(d).wait_send()
            sel_copy.wait_send()

    return drain


def decode_kernel(
    w_copies, durations, assign, we, sel, params,
    out, wm, flat, xe, entry, xp, prod, fine, tails, rows, spread, permute,
):
    f32, bf16 = jnp.float32, jnp.bfloat16
    lane = lax.broadcasted_iota(jnp.int32, (1, CELLS), 1)
    cell_r, cell_q = lane // WT, lane % WT
    diagonal = lax.broadcasted_iota(jnp.int32, (COUT, COUT), 0) == lax.broadcasted_iota(jnp.int32, (COUT, COUT), 1)

    def column(ref):
        return jnp.sum(jnp.where(diagonal, ref, 0.0), axis=1, keepdims=True)

    bias_col, gain_col, shift_col = (column(params[n]) for n in range(3, 6))
    own = assign[lax.axis_index("tile")]
    duration_of = (durations[own], durations[jnp.maximum(own - 1, 0)])
    groups = COUT // GSIZE

    def frame(f):
        return slice(f * CELLS, (f + 1) * CELLS)

    def add_live(terms, duration):
        total = terms[0]
        for f in range(1, FT):
            total = total + (terms[f] if f < FT // 2 else terms[f] * (f < duration).astype(f32))
        return total

    def im2col(j):
        flat[...] = sel[j].astype(f32).reshape(CL * FT, CELLS)
        base = jnp.concatenate([flat[pl.ds(f, CL, stride=FT), :] for f in range(FT)], axis=0)
        for s in range(9):
            b, c = s // 3 - 1, s % 3 - 1
            moved = base
            if s != 4:
                moved = pltpu.roll(base, (-(b * WT + c)) % CELLS, 1)
                inside = (cell_r + b >= 0) & (cell_r + b < CELLS // WT) & (cell_q + c >= 0) & (cell_q + c < WT)
                moved = jnp.where(inside, moved, 0.0)
            moved = moved.astype(bf16)
            for a in range(3):
                for f in range(FT):
                    at = max(f - 2 + a, 0)
                    xe[j, (9 * a + s) * CL:(9 * a + s + 1) * CL, frame(f)] = moved[at * CL:(at + 1) * CL]

    chunks = [slice(i * COUT, (i + 1) * COUT) for i in range(CIN // COUT)]
    pairs = range(FT // 2)

    def pair(n):
        return slice(n * 2 * CELLS, (n + 1) * 2 * CELLS)

    def enter(j, n):
        entry[j, :, pair(n)] = jnp.dot(we[...], xe[j, :, pair(n)], preferred_element_type=f32)

    def group_sum(x, members):
        return jnp.sum(x.reshape(groups, GSIZE, CELLS), axis=(1, 2), keepdims=True) * members

    def spread_rows(x):
        return jnp.broadcast_to(x, (groups, GSIZE, 1)).reshape(COUT, 1)

    means, scales, coefs = {}, {}, {}
    members = [1.0 / (GSIZE * CELLS * d.astype(f32)) for d in duration_of]

    def mean_of(j, i):
        total = add_live([entry[j, chunks[i], frame(f)] for f in range(FT)], duration_of[j])
        means[j, i] = spread_rows(group_sum(total, members[j]))

    def scale_of(j, i):
        squares = []
        for f in range(FT):
            centred = entry[j, chunks[i], frame(f)] - means[j, i]
            squares.append(centred * centred)
        var = group_sum(add_live(squares, duration_of[j]), members[j])
        scales[j, i] = spread_rows(0.5 * lax.rsqrt(var + EPS))

    def coef_of(i):
        start = WROWS + 3 - (KE - CELLS)
        extra = we[chunks[i], KE - CELLS:].astype(f32)
        g1 = jnp.sum(jnp.where((lane >= start) & (lane < start + 3), extra, 0.0), axis=1, keepdims=True)
        b1 = jnp.sum(jnp.where((lane >= start + 3) & (lane < start + 6), extra, 0.0), axis=1, keepdims=True)
        coefs[i] = g1, b1

    def normalise(j, n):
        for i, at in enumerate(chunks):
            g1, b1 = coefs[i]
            scale = scales[j, i] * g1
            offset = 0.5 * b1 - means[j, i] * scale
            for f in (2 * n, 2 * n + 1):
                half = entry[j, at, frame(f)] * scale + offset
                coarse = (half * jnp.tanh(half) + half).astype(bf16)
                xp[j, at, frame(f + 2)] = coarse
                if f == 0:
                    xp[j, at, frame(0)] = coarse
                    xp[j, at, frame(1)] = coarse

    top, bottom = cell_r >= 1, cell_r < CELLS // WT - 1
    left, right = cell_q >= 1, cell_q < WT - 1

    def mix(j, n):
        first = n * 2 * CELLS
        delayed = jnp.concatenate(
            [xp[j, :, first + a * CELLS:first + (a + 2) * CELLS] for a in range(3)], axis=0
        )
        prod[j, :, pair(n)] = jnp.dot(wm[...], delayed, preferred_element_type=f32)

    sums = {}

    def upsample(j, n):
        for f in (2 * n, 2 * n + 1):
            p = [prod[j, s * COUT:(s + 1) * COUT, frame(f)] for s in range(9)]
            p[4] = p[4] + bias_col
            upper, lower = [], []
            for c in range(3):
                upper.append(jnp.where(top, pltpu.roll(p[c], WT, 1), 0.0) + (p[3 + c] + p[6 + c]))
                lower.append((p[c] + p[3 + c]) + jnp.where(bottom, pltpu.roll(p[6 + c], CELLS - WT, 1), 0.0))
            phases = []
            for r in (upper, lower):
                phases.append(jnp.where(left, pltpu.roll(r[0], 1, 1), 0.0) + (r[1] + r[2]))
                phases.append((r[0] + r[1]) + jnp.where(right, pltpu.roll(r[2], CELLS - 1, 1), 0.0))
            for m in range(4):
                fine[j, f, :, frame(m)] = phases[m]
            sums[j, f] = (phases[0] + phases[1]) + (phases[2] + phases[3])

    def finisher(j):
        members = 1.0 / (GSIZE * 4 * CELLS * duration_of[j].astype(f32))
        mean = spread_rows(group_sum(add_live([sums[j, f] for f in range(FT)], duration_of[j]), members))
        squares = []
        for f in range(FT):
            total = None
            for n in range(4):
                centred = fine[j, f, :, frame(n)] - mean
                total = centred * centred if total is None else total + centred * centred
            squares.append(total)
        var = group_sum(add_live(squares, duration_of[j]), members)
        scale = gain_col * spread_rows(0.5 * lax.rsqrt(var + EPS))
        offset = 0.5 * shift_col - mean * scale

        def finish(f):
            half = fine[j, f] * scale + offset
            return (half * jnp.tanh(half) + half).astype(bf16)

        return finish

    im2col(1)
    im2col(0)
    for n in pairs:
        enter(1, n)
    for i in range(len(chunks)):
        mean_of(1, i)
        coef_of(i)
        if i % 2:
            enter(0, i // 2)
    for i in range(len(chunks)):
        scale_of(1, i)
    normalise(1, 0)
    for copy in w_copies:
        copy.wait()
    for n in pairs:
        mix(1, n)
        if n + 1 < len(pairs):
            normalise(1, n + 1)
        for i in (2 * n, 2 * n + 1):
            mean_of(0, i)
        if n > 0:
            upsample(1, n - 1)
    for i in range(len(chunks)):
        scale_of(0, i)
    normalise(0, 0)
    for n in pairs:
        mix(0, n)
        if n + 1 < len(pairs):
            normalise(0, n + 1)
        if n == 0:
            upsample(1, len(pairs) - 1)
        if n == 1:
            finish = finisher(1)
            for k in range(OV):
                tails[k] = finish(jnp.clip(duration_of[1] - OV + k, 0, FT - 1))
        if n > 0:
            upsample(0, n - 1)
    upsample(0, len(pairs) - 1)
    finish = finisher(0)
    for f in range(FT):
        result = finish(f).astype(f32)
        if f >= FT // 2:
            result = jnp.where(f < duration_of[0], result, 0.0)
        if f < OV:
            w = (f + 1) / (OV + 1)
            blended = result * w + tails[f].astype(f32) * (1.0 - w)
            result = jnp.where(own == 0, result, blended)
        rows[f * COUT:(f + 1) * COUT, :] = result.astype(bf16)

    whole = jnp.dot(rows[...], permute[...], preferred_element_type=f32)
    for f in range(FT):
        for n in range(4):
            spread[n, pl.ds(f, COUT, stride=FT), :] = whole[f * COUT:(f + 1) * COUT, frame(n)]
    for n in range(4):
        out[:, :, frame(n)] = spread[n].astype(bf16).reshape(COUT, FT, CELLS)


def prepare(xe, permute):
    last = lax.broadcasted_iota(jnp.int32, (KE - WROWS, FT * CELLS), 0)
    ones = jnp.where(last < 3, 1.0, 0.0).astype(jnp.bfloat16)
    for j in range(2):
        xe[j, WROWS:, :] = ones
    col = lax.broadcasted_iota(jnp.int32, (1, 4 * CELLS), 1)
    fr, fc = col // (2 * WT), col % (2 * WT)
    source = ((fr % 2) * 2 + fc % 2) * CELLS + (fr // 2) * WT + fc // 2
    found = lax.broadcasted_iota(jnp.int32, (4 * CELLS, 4 * CELLS), 0) == source
    permute[...] = found.astype(jnp.float32).astype(jnp.bfloat16)


def fused_kernel(
    tiles, chans,
    durations_in, assign_in, lat, wt, bias1, gain1, shift1, w3, bias2, gain2, shift2,
    out,
    durations, assign, params, we, sel, ext, stage,
    wm, flat, xe, entry, xp, prod, fine, tails, rows, spread, permute,
    s_lat, r_lat, s_z, r_z, s_sib, r_sib, s_sel, r_sel, ready, w_sem, load_sem,
):
    me_t = lax.axis_index("tile")
    loads = [pltpu.make_async_copy(wt, ext.at[:WROWS], load_sem.at[0])]
    for n, ref in enumerate((bias1, gain1, shift1, bias2, gain2, shift2)):
        loads.append(pltpu.make_async_copy(ref, params.at[n], load_sem.at[n + 1]))
    loads.append(pltpu.make_async_copy(durations_in, durations, load_sem.at[7]))
    loads.append(pltpu.make_async_copy(assign_in, assign, load_sem.at[8]))
    own_copy = pltpu.make_async_copy(lat, stage.at[me_t], load_sem.at[9])
    w_copies = [
        pltpu.make_async_copy(w3.at[a], wm.at[:, a * CIN:(a + 1) * CIN], w_sem.at[a]) for a in range(3)
    ]

    def start_loads():
        for copy in loads + w_copies:
            copy.start()

    drain = gather_kernel(
        tiles, chans, lambda: prepare(xe, permute), start_loads, loads, own_copy, assign, lat, params, we, sel, ext, stage,
        s_lat, r_lat, s_z, r_z, s_sib, r_sib, s_sel, r_sel, ready,
    )
    decode_kernel(
        w_copies, durations, assign, we, sel, params,
        out, wm, flat, xe, entry, xp, prod, fine, tails, rows, spread, permute,
    )
    drain()


def fused(tiles, chans, *args):
    vmem = pl.BlockSpec(memory_space=pltpu.VMEM)
    hbm = pl.BlockSpec(memory_space=pl.ANY)
    dma = pltpu.SemaphoreType.DMA
    bf16, f32 = jnp.bfloat16, jnp.float32
    return pl.pallas_call(
        functools.partial(fused_kernel, tiles, chans),
        out_shape=pltpu.VMEM((COUT, FT, 4 * CELLS), bf16),
        in_specs=[hbm] * 11,
        out_specs=vmem,
        scratch_shapes=[
            pltpu.SMEM((tiles,), jnp.int32),
            pltpu.SMEM((tiles,), jnp.int32),
            pltpu.VMEM((6, 1, COUT), f32),
            pltpu.VMEM((CIN, KE), bf16),
            pltpu.VMEM((2, CL, FT, CELLS), bf16),
            pltpu.VMEM((KE, COUT), bf16),
            pltpu.VMEM((tiles, CL, FT, CELLS), bf16),
            pltpu.VMEM((9 * COUT, 3 * CIN), bf16),
            pltpu.VMEM((CL * FT, CELLS), f32),
            pltpu.VMEM((2, KE, FT * CELLS), bf16),
            pltpu.VMEM((2, CIN, FT * CELLS), f32),
            pltpu.VMEM((2, CIN, (FT + 2) * CELLS), bf16),
            pltpu.VMEM((2, 9 * COUT, FT * CELLS), f32),
            pltpu.VMEM((2, FT, COUT, 4 * CELLS), f32),
            pltpu.VMEM((OV, COUT, 4 * CELLS), bf16),
            pltpu.VMEM((FT * COUT, 4 * CELLS), bf16),
            pltpu.VMEM((4, FT * COUT, CELLS), f32),
            pltpu.VMEM((4 * CELLS, 4 * CELLS), bf16),
            dma((tiles - 1,)), dma((tiles - 1,)),
            dma((3,)), dma((3,)),
            dma((4,)), dma((4,)),
            dma, dma, pltpu.SemaphoreType.REGULAR,
            dma((3,)),
            dma((10,)),
        ],
        compiler_params=pltpu.CompilerParams(
            collective_id=0, has_side_effects=True, vmem_limit_bytes=56 * 1024 * 1024
        ),
    )(*args)


def solution(mesh):
    tiles, chans = mesh.shape["tile"], mesh.shape["chan"]

    def local(latents, durations, assignment, entry_weight, entry_bias, first_gain, first_shift,
              mixer_weight, mixer_bias, second_gain, second_shift):
        wt = jnp.transpose(entry_weight, (0, 2, 1)).reshape(WROWS, COUT)
        out = fused(
            tiles, chans, durations, assignment, latents[0], wt, entry_bias[None], first_gain[None],
            first_shift[None], mixer_weight.reshape(3, 9 * COUT, CIN), mixer_bias[None], second_gain[None],
            second_shift[None],
        )
        return out[None]

    in_specs = (
        P("tile", None, None, None), P(), P(), P(None, "chan", None), P("chan"), P("chan"), P("chan"),
        P(None, "chan", None), P("chan"), P("chan"), P("chan"),
    )
    return jax.shard_map(
        local, mesh=mesh, in_specs=in_specs, out_specs=P("tile", "chan", None, None), check_vma=False
    )
```

```python
import functools

import jax
import jax.numpy as jnp
from jax import lax
from jax.experimental import pallas as pl
from jax.experimental.pallas import tpu as pltpu
from jax.sharding import PartitionSpec as P

MESH = pl.DeviceIdType.MESH
GSIZE = 16
OV = 3
FT = 8
WT = 16
CELLS = 128
CL = 16
COUT = 64
CIN = 512
KE = 512
WROWS = 432
EARLY = 3
SIDE = 4
HALF = CL // 2
LATE = 2
EPS = 1e-06


def three_parts(x):
    hi = x.astype(jnp.bfloat16).astype(jnp.float32)
    rest = x - hi
    mid = rest.astype(jnp.bfloat16).astype(jnp.float32)
    return hi, mid, rest - mid


def gather_kernel(
    tiles, chans, prepare_rest, start_loads, loads, own_copies,
    assign, lat, params,
    we, sel,
    ext, near, far_out, far_in,
    s_lat, r_lat, s_z, r_z, s_sib, r_sib, s_sel, r_sel, ready,
):
    me_t = lax.axis_index("tile")
    me_c = lax.axis_index("chan")
    z, core = me_c // 2, me_c % 2
    zs = chans // 2
    sibling = (me_t, z * 2 + 1 - core)

    place = (me_t % SIDE, me_t // SIDE)

    def along(axis, d):
        x, y = place
        return y * SIDE + (x + d) % SIDE if axis == 0 else ((y + d) % SIDE) * SIDE + x

    barrier = pltpu.get_barrier_semaphore()

    @pl.when(core == 0)
    def _():
        for d in range(1, zs):
            pl.semaphore_signal(barrier, inc=1, device_id=(me_t, ((z + d) % zs) * 2), device_id_type=MESH)

    @pl.when(core == 1)
    def _():
        for d in range(zs):
            pl.semaphore_signal(barrier, inc=1, device_id=(me_t, ((z + d) % zs) * 2), device_id_type=MESH)
        for axis in range(2):
            for d in range(1, SIDE):
                pl.semaphore_signal(barrier, inc=1, device_id=(along(axis, d), me_c), device_id_type=MESH)

    start_loads()

    def shard(chip, half):
        return pl.ds(pl.multiple_of((chip * 2 + half) * COUT, COUT), COUT)

    def pack_weights():
        for copy in loads:
            copy.wait()
        row = lax.broadcasted_iota(jnp.int32, (16, COUT), 0)
        packed = jnp.zeros((16, COUT), jnp.float32)
        for n in range(3):
            for at, piece in enumerate(three_parts(params[n])):
                packed = jnp.where(row == 3 * n + at, piece, packed)
        ext[WROWS:WROWS + 16, :] = packed.astype(jnp.bfloat16)
        ext[WROWS + 16:, :] = jnp.zeros((KE - WROWS - 16, COUT), jnp.bfloat16)
        eye = (
            lax.broadcasted_iota(jnp.int32, (COUT, COUT), 0)
            == lax.broadcasted_iota(jnp.int32, (COUT, COUT), 1)
        ).astype(jnp.bfloat16)

        we[shard(z, core), :] = lax.dot_general(
            eye, ext[...], (((1,), (1,)), ((), ())), preferred_element_type=jnp.float32
        ).astype(jnp.bfloat16)

    def first_copy(h, d):
        return pltpu.make_async_remote_copy(
            src_ref=lat.at[pl.ds(h * HALF, HALF)], dst_ref=near[h].at[place[h]],
            send_sem=s_lat.at[0, h, d - 1], recv_sem=r_lat.at[0, h, d - 1],
            device_id=(along(h, d), me_c), device_id_type=MESH,
        )

    def second_copy(h, d):
        return pltpu.make_async_remote_copy(
            src_ref=far_out.at[h, d - 1], dst_ref=far_in[h].at[place[1 - h]],
            send_sem=s_lat.at[1, h, d - 1], recv_sem=r_lat.at[1, h, d - 1],
            device_id=(along(1 - h, d), me_c), device_id_type=MESH,
        )

    def wanted(slot):
        own = assign[slot]
        return own, jnp.maximum(own - 1, 0)

    def spot(axis, tile):
        return tile % SIDE if axis == 0 else tile // SIDE

    def z_copy(d):
        rows = shard(z, core)
        return pltpu.make_async_remote_copy(
            src_ref=we.at[rows], dst_ref=we.at[rows],
            send_sem=s_z.at[d - 1], recv_sem=r_z.at[d - 1],
            device_id=(me_t, ((z + d) % zs) * 2 + core), device_id_type=MESH,
        )

    def sib_copy(d):
        rows = shard((z + zs - d) % zs, core)
        return pltpu.make_async_remote_copy(
            src_ref=we.at[rows], dst_ref=we.at[rows],
            send_sem=s_sib.at[d], recv_sem=r_sib.at[d],
            device_id=sibling, device_id_type=MESH,
        )

    def send_own():
        for d in order:
            z_copy(d).start()
        sib_copy(0).start()

    def hand_on():
        for d in order:
            z_copy(d).wait_recv()
            sib_copy(d).start()

    def finish_weights():
        for d in range(zs):
            sib_copy(d).wait_recv()

    sel_copy = pltpu.make_async_remote_copy(
        src_ref=sel, dst_ref=sel, send_sem=s_sel, recv_sem=r_sel, device_id=sibling, device_id_type=MESH,
    )
    order = (2, 1, zs - 1)
    turns = (2, 1, SIDE - 1)

    @pl.when(core == 0)
    def _():
        def meet():
            pl.semaphore_wait(barrier, chans - 1)
            pl.semaphore_signal(ready, inc=1, device_id=sibling, device_id_type=MESH)

        @pl.when(z < LATE)
        def _():
            pack_weights()
            meet()

        @pl.when(z >= LATE)
        def _():
            meet()
            pack_weights()

        send_own()
        prepare_rest()
        hand_on()
        finish_weights()
        sel_copy.wait_recv()

    @pl.when(core == 1)
    def _():
        for copy in own_copies:
            copy.start()

        def send_weights():
            pl.semaphore_wait(ready, 1)
            send_own()

        def send_latents():
            pl.semaphore_wait(barrier, 2 * (SIDE - 1))
            for d in turns:
                for h in range(2):
                    first_copy(h, d).start()

        first = z < EARLY

        @pl.when(first)
        def _():
            send_latents()
            pack_weights()
            send_weights()

        @pl.when(jnp.logical_not(first))
        def _():
            pack_weights()
            send_weights()
            send_latents()

        prepare_rest()
        for copy in own_copies:
            copy.wait()
        for h in range(2):
            for d in turns:
                first_copy(h, d).wait_recv()
            for d in turns:
                for j, tile in enumerate(wanted(along(1 - h, d))):
                    far_out[h, d - 1, j] = near[h][spot(h, tile)]
                second_copy(h, d).start()
            for j, tile in enumerate(wanted(me_t)):
                far_in[h][place[1 - h], j] = near[h][spot(h, tile)]
        for h in range(2):
            for d in turns:
                second_copy(h, d).wait_recv()
            for j, tile in enumerate(wanted(me_t)):
                sel[j, h * HALF:(h + 1) * HALF] = far_in[h][spot(1 - h, tile), j]
        sel_copy.start()
        hand_on()
        finish_weights()

    def drain():
        for d in order:
            z_copy(d).wait_send()
        for d in range(zs):
            sib_copy(d).wait_send()

        @pl.when(core == 1)
        def _():
            for h in range(2):
                for d in turns:
                    first_copy(h, d).wait_send()
                    second_copy(h, d).wait_send()
            sel_copy.wait_send()

    return drain


def decode_kernel(
    w_copies, durations, assign, we, sel, params,
    out, wm, flat, xe, entry, xp, prod, fine, tails, spread, permute,
):
    f32, bf16 = jnp.float32, jnp.bfloat16
    lane = lax.broadcasted_iota(jnp.int32, (1, CELLS), 1)
    cell_r, cell_q = lane // WT, lane % WT
    diagonal = lax.broadcasted_iota(jnp.int32, (COUT, COUT), 0) == lax.broadcasted_iota(jnp.int32, (COUT, COUT), 1)

    def column(ref):
        return jnp.sum(jnp.where(diagonal, ref, 0.0), axis=1, keepdims=True)

    bias_col, gain_col, shift_col = (column(params[n]) for n in range(3, 6))
    own = assign[lax.axis_index("tile")]
    duration_of = (durations[own], durations[jnp.maximum(own - 1, 0)])
    groups = COUT // GSIZE

    def frame(f):
        return slice(f * CELLS, (f + 1) * CELLS)

    def add_live(terms, duration):
        total = terms[0]
        for f in range(1, FT):
            total = total + (terms[f] if f < FT // 2 else terms[f] * (f < duration).astype(f32))
        return total

    def im2col(j):
        flat[...] = sel[j].astype(f32).reshape(CL * FT, CELLS)
        base = jnp.concatenate([flat[pl.ds(f, CL, stride=FT), :] for f in range(FT)], axis=0)
        for s in range(9):
            b, c = s // 3 - 1, s % 3 - 1
            moved = base
            if s != 4:
                moved = pltpu.roll(base, (-(b * WT + c)) % CELLS, 1)
                inside = (cell_r + b >= 0) & (cell_r + b < CELLS // WT) & (cell_q + c >= 0) & (cell_q + c < WT)
                moved = jnp.where(inside, moved, 0.0)
            moved = moved.astype(bf16)
            for a in range(3):
                for f in range(FT):
                    at = max(f - 2 + a, 0)
                    xe[j, (9 * a + s) * CL:(9 * a + s + 1) * CL, frame(f)] = moved[at * CL:(at + 1) * CL]

    chunks = [slice(i * COUT, (i + 1) * COUT) for i in range(CIN // COUT)]
    pairs = range(FT // 2)

    def pair(n):
        return slice(n * 2 * CELLS, (n + 1) * 2 * CELLS)

    def enter(j, n):
        entry[j, :, pair(n)] = jnp.dot(we[...], xe[j, :, pair(n)], preferred_element_type=f32)

    def group_sum(x, members):
        return jnp.sum(x.reshape(groups, GSIZE, CELLS), axis=(1, 2), keepdims=True) * members

    def spread_rows(x):
        return jnp.broadcast_to(x, (groups, GSIZE, 1)).reshape(COUT, 1)

    means, scales, coefs = {}, {}, {}
    members = [1.0 / (GSIZE * CELLS * d.astype(f32)) for d in duration_of]

    def mean_of(j, i):
        total = add_live([entry[j, chunks[i], frame(f)] for f in range(FT)], duration_of[j])
        means[j, i] = spread_rows(group_sum(total, members[j]))

    def scale_of(j, i):
        squares = []
        for f in range(FT):
            centred = entry[j, chunks[i], frame(f)] - means[j, i]
            squares.append(centred * centred)
        var = group_sum(add_live(squares, duration_of[j]), members[j])
        scales[j, i] = spread_rows(0.5 * lax.rsqrt(var + EPS))

    def coef_of(i):
        start = WROWS + 3 - (KE - CELLS)
        extra = we[chunks[i], KE - CELLS:].astype(f32)
        g1 = jnp.sum(jnp.where((lane >= start) & (lane < start + 3), extra, 0.0), axis=1, keepdims=True)
        b1 = jnp.sum(jnp.where((lane >= start + 3) & (lane < start + 6), extra, 0.0), axis=1, keepdims=True)
        coefs[i] = g1, b1

    def normalise(j, n):
        for i, at in enumerate(chunks):
            g1, b1 = coefs[i]
            scale = scales[j, i] * g1
            offset = 0.5 * b1 - means[j, i] * scale
            for f in (2 * n, 2 * n + 1):
                half = entry[j, at, frame(f)] * scale + offset
                coarse = (half * jnp.tanh(half) + half).astype(bf16)
                xp[j, at, frame(f + 2)] = coarse
                if f == 0:
                    xp[j, at, frame(0)] = coarse
                    xp[j, at, frame(1)] = coarse

    top, bottom = cell_r >= 1, cell_r < CELLS // WT - 1
    left, right = cell_q >= 1, cell_q < WT - 1

    def mix(j, n):
        first = n * 2 * CELLS
        delayed = jnp.concatenate(
            [xp[j, :, first + a * CELLS:first + (a + 2) * CELLS] for a in range(3)], axis=0
        )
        prod[j, :, pair(n)] = jnp.dot(wm[...], delayed, preferred_element_type=f32)

    sums, squares, pivots = {}, {}, {}

    def upsample(j, n):
        for f in (2 * n, 2 * n + 1):
            p = [prod[j, s * COUT:(s + 1) * COUT, frame(f)] for s in range(9)]
            p[4] = p[4] + bias_col
            upper, lower = [], []
            for c in range(3):
                upper.append(jnp.where(top, pltpu.roll(p[c], WT, 1), 0.0) + (p[3 + c] + p[6 + c]))
                lower.append((p[c] + p[3 + c]) + jnp.where(bottom, pltpu.roll(p[6 + c], CELLS - WT, 1), 0.0))
            phases = []
            for r in (upper, lower):
                phases.append(jnp.where(left, pltpu.roll(r[0], 1, 1), 0.0) + (r[1] + r[2]))
                phases.append((r[0] + r[1]) + jnp.where(right, pltpu.roll(r[2], CELLS - 1, 1), 0.0))
            for m in range(4):
                fine[j, f, :, frame(m)] = phases[m]
            sums[j, f] = (phases[0] + phases[1]) + (phases[2] + phases[3])
        if n == 0:
            pivots[j] = spread_rows(group_sum(sums[j, 0] + sums[j, 1], 1.0 / (GSIZE * 8 * CELLS)))
        for f in (2 * n, 2 * n + 1):
            total = None
            for m in range(4):
                apart = fine[j, f, :, frame(m)] - pivots[j]
                total = apart * apart if total is None else total + apart * apart
            squares[j, f] = total

    def finisher(j):
        members = 1.0 / (GSIZE * 4 * CELLS * duration_of[j].astype(f32))
        mean = group_sum(add_live([sums[j, f] for f in range(FT)], duration_of[j]), members)
        about = group_sum(add_live([squares[j, f] for f in range(FT)], duration_of[j]), members)
        mean = spread_rows(mean)
        off = mean - pivots[j]
        var = jnp.maximum(spread_rows(about) - off * off, 0.0)
        scale = gain_col * (0.5 * lax.rsqrt(var + EPS))
        offset = 0.5 * shift_col - mean * scale

        def finish(f, at=slice(None)):
            half = fine[j, f, at] * scale[at] + offset[at]
            return (half * jnp.tanh(half) + half).astype(bf16)

        return finish

    im2col(1)
    im2col(0)
    for n in pairs:
        enter(1, n)
    for i in range(len(chunks)):
        mean_of(1, i)
        coef_of(i)
        if i % 2:
            enter(0, i // 2)
    for i in range(len(chunks)):
        scale_of(1, i)
    normalise(1, 0)
    for copy in w_copies:
        copy.wait()
    for n in pairs:
        mix(1, n)
        if n + 1 < len(pairs):
            normalise(1, n + 1)
        for i in (2 * n, 2 * n + 1):
            mean_of(0, i)
        if n > 0:
            upsample(1, n - 1)
    for i in range(len(chunks)):
        scale_of(0, i)
    normalise(0, 0)
    for n in pairs:
        mix(0, n)
        if n + 1 < len(pairs):
            normalise(0, n + 1)
        if n == 0:
            upsample(1, len(pairs) - 1)
        if n == 1:
            finish = finisher(1)
            for k in range(OV):
                tails[k] = finish(jnp.clip(duration_of[1] - OV + k, 0, FT - 1))
        if n > 0:
            upsample(0, n - 1)
    upsample(0, len(pairs) - 1)
    finish = finisher(0)
    part = COUT // 2
    for at in (slice(0, part), slice(part, COUT)):
        for f in range(FT):
            result = finish(f, at).astype(f32)
            if f >= FT // 2:
                result = jnp.where(f < duration_of[0], result, 0.0)
            if f < OV:
                w = (f + 1) / (OV + 1)
                blended = result * w + tails[f, at].astype(f32) * (1.0 - w)
                result = jnp.where(own == 0, result, blended)
            for n in range(4):
                spread[n, pl.ds(at.start * FT + f, part, stride=FT), :] = result[:, frame(n)]
        whole = slice(at.start * FT, at.stop * FT)
        rows = jnp.concatenate([spread[n, whole, :].astype(bf16) for n in range(4)], axis=1)
        moved = jnp.dot(rows, permute[...], preferred_element_type=f32)
        out[at] = moved.astype(bf16).reshape(part, FT, 4 * CELLS)


def prepare(xe, permute):
    last = lax.broadcasted_iota(jnp.int32, (KE - WROWS, FT * CELLS), 0)
    ones = jnp.where(last < 3, 1.0, 0.0).astype(jnp.bfloat16)
    for j in range(2):
        xe[j, WROWS:, :] = ones
    col = lax.broadcasted_iota(jnp.int32, (1, 4 * CELLS), 1)
    fr, fc = col // (2 * WT), col % (2 * WT)
    source = ((fr % 2) * 2 + fc % 2) * CELLS + (fr // 2) * WT + fc // 2
    found = lax.broadcasted_iota(jnp.int32, (4 * CELLS, 4 * CELLS), 0) == source
    permute[...] = found.astype(jnp.float32).astype(jnp.bfloat16)


def fused_kernel(
    tiles, chans,
    durations_in, assign_in, lat, wt, bias1, gain1, shift1, w3, bias2, gain2, shift2,
    out,
    durations, assign, params, we, sel, ext, near0, near1, far_out, far_in0, far_in1,
    wm, flat, xe, entry, xp, prod, fine, tails, spread, permute,
    s_lat, r_lat, s_z, r_z, s_sib, r_sib, s_sel, r_sel, ready, w_sem, load_sem,
):
    me_t = lax.axis_index("tile")
    loads = [pltpu.make_async_copy(wt, ext.at[:WROWS], load_sem.at[0])]
    for n, ref in enumerate((bias1, gain1, shift1, bias2, gain2, shift2)):
        loads.append(pltpu.make_async_copy(ref, params.at[n], load_sem.at[n + 1]))
    loads.append(pltpu.make_async_copy(durations_in, durations, load_sem.at[7]))
    loads.append(pltpu.make_async_copy(assign_in, assign, load_sem.at[8]))
    near, far_in = (near0, near1), (far_in0, far_in1)
    own_copies = [
        pltpu.make_async_copy(lat.at[pl.ds(h * HALF, HALF)], near[h].at[place], load_sem.at[9 + h])
        for h, place in enumerate((me_t % SIDE, me_t // SIDE))
    ]
    w_copies = [
        pltpu.make_async_copy(w3.at[a], wm.at[:, a * CIN:(a + 1) * CIN], w_sem.at[a]) for a in range(3)
    ]

    def start_loads():
        for copy in loads + w_copies:
            copy.start()

    drain = gather_kernel(
        tiles, chans, lambda: prepare(xe, permute), start_loads, loads, own_copies, assign, lat, params, we, sel, ext,
        near, far_out, far_in,
        s_lat, r_lat, s_z, r_z, s_sib, r_sib, s_sel, r_sel, ready,
    )
    decode_kernel(
        w_copies, durations, assign, we, sel, params,
        out, wm, flat, xe, entry, xp, prod, fine, tails, spread, permute,
    )
    drain()


def fused(tiles, chans, *args):
    vmem = pl.BlockSpec(memory_space=pltpu.VMEM)
    hbm = pl.BlockSpec(memory_space=pl.ANY)
    dma = pltpu.SemaphoreType.DMA
    bf16, f32 = jnp.bfloat16, jnp.float32
    return pl.pallas_call(
        functools.partial(fused_kernel, tiles, chans),
        out_shape=pltpu.VMEM((COUT, FT, 4 * CELLS), bf16),
        in_specs=[hbm] * 11,
        out_specs=vmem,
        scratch_shapes=[
            pltpu.SMEM((tiles,), jnp.int32),
            pltpu.SMEM((tiles,), jnp.int32),
            pltpu.VMEM((6, 1, COUT), f32),
            pltpu.VMEM((CIN, KE), bf16),
            pltpu.VMEM((2, CL, FT, CELLS), bf16),
            pltpu.VMEM((KE, COUT), bf16),
            *[pltpu.VMEM((SIDE, HALF, FT, CELLS), bf16)] * 2,
            pltpu.VMEM((2, SIDE - 1, 2, HALF, FT, CELLS), bf16),
            *[pltpu.VMEM((SIDE, 2, HALF, FT, CELLS), bf16)] * 2,
            pltpu.VMEM((9 * COUT, 3 * CIN), bf16),
            pltpu.VMEM((CL * FT, CELLS), f32),
            pltpu.VMEM((2, KE, FT * CELLS), bf16),
            pltpu.VMEM((2, CIN, FT * CELLS), f32),
            pltpu.VMEM((2, CIN, (FT + 2) * CELLS), bf16),
            pltpu.VMEM((2, 9 * COUT, FT * CELLS), f32),
            pltpu.VMEM((2, FT, COUT, 4 * CELLS), f32),
            pltpu.VMEM((OV, COUT, 4 * CELLS), bf16),
            pltpu.VMEM((4, FT * COUT, CELLS), f32),
            pltpu.VMEM((4 * CELLS, 4 * CELLS), bf16),
            dma((2, 2, SIDE - 1)), dma((2, 2, SIDE - 1)),
            dma((3,)), dma((3,)),
            dma((4,)), dma((4,)),
            dma, dma, pltpu.SemaphoreType.REGULAR,
            dma((3,)),
            dma((11,)),
        ],
        compiler_params=pltpu.CompilerParams(
            collective_id=0, has_side_effects=True, vmem_limit_bytes=56 * 1024 * 1024
        ),
    )(*args)


def solution(mesh):
    tiles, chans = mesh.shape["tile"], mesh.shape["chan"]

    def local(latents, durations, assignment, entry_weight, entry_bias, first_gain, first_shift,
              mixer_weight, mixer_bias, second_gain, second_shift):
        wt = jnp.transpose(entry_weight, (0, 2, 1)).reshape(WROWS, COUT)
        out = fused(
            tiles, chans, durations, assignment, latents[0], wt, entry_bias[None], first_gain[None],
            first_shift[None], mixer_weight.reshape(3, 9 * COUT, CIN), mixer_bias[None], second_gain[None],
            second_shift[None],
        )
        return out[None]

    in_specs = (
        P("tile", None, None, None), P(), P(), P(None, "chan", None), P("chan"), P("chan"), P("chan"),
        P(None, "chan", None), P("chan"), P("chan"), P("chan"),
    )
    return jax.shard_map(
        local, mesh=mesh, in_specs=in_specs, out_specs=P("tile", "chan", None, None), check_vma=False
    )
```

```python
import functools

import jax
import jax.numpy as jnp
from jax import lax
from jax.experimental import pallas as pl
from jax.experimental.pallas import tpu as pltpu
from jax.sharding import PartitionSpec as P

MESH = pl.DeviceIdType.MESH
GSIZE = 16
OV = 3
FT = 8
WT = 16
CELLS = 128
CL = 16
COUT = 64
CIN = 512
KE = 512
WROWS = 432
EARLY = 3
SIDE = 4
HALF = CL // 2
LATE = 2
EPS = 1e-06


def three_parts(x):
    hi = x.astype(jnp.bfloat16).astype(jnp.float32)
    rest = x - hi
    mid = rest.astype(jnp.bfloat16).astype(jnp.float32)
    return hi, mid, rest - mid


def gather_kernel(
    tiles, chans, prepare_rest, start_loads, loads, own_copies,
    assign, lat, params,
    we, sel,
    ext, near, far_out, far_in,
    s_lat, r_lat, s_z, r_z, s_sib, r_sib, s_sel, r_sel, ready,
):
    me_t = lax.axis_index("tile")
    me_c = lax.axis_index("chan")
    z, core = me_c // 2, me_c % 2
    zs = chans // 2
    sibling = (me_t, z * 2 + 1 - core)

    place = (me_t % SIDE, me_t // SIDE)

    def along(axis, d):
        x, y = place
        return y * SIDE + (x + d) % SIDE if axis == 0 else ((y + d) % SIDE) * SIDE + x

    barrier = pltpu.get_barrier_semaphore()

    @pl.when(core == 0)
    def _():
        for d in range(1, zs):
            pl.semaphore_signal(barrier, inc=1, device_id=(me_t, ((z + d) % zs) * 2), device_id_type=MESH)

    @pl.when(core == 1)
    def _():
        for d in range(zs):
            pl.semaphore_signal(barrier, inc=1, device_id=(me_t, ((z + d) % zs) * 2), device_id_type=MESH)
        for axis in range(2):
            for d in range(1, SIDE):
                pl.semaphore_signal(barrier, inc=1, device_id=(along(axis, d), me_c), device_id_type=MESH)

    start_loads()

    def shard(chip, half):
        return pl.ds(pl.multiple_of((chip * 2 + half) * COUT, COUT), COUT)

    def pack_weights():
        for copy in loads:
            copy.wait()
        row = lax.broadcasted_iota(jnp.int32, (16, COUT), 0)
        packed = jnp.zeros((16, COUT), jnp.float32)
        for n in range(3):
            for at, piece in enumerate(three_parts(params[n])):
                packed = jnp.where(row == 3 * n + at, piece, packed)
        ext[WROWS:WROWS + 16, :] = packed.astype(jnp.bfloat16)
        ext[WROWS + 16:, :] = jnp.zeros((KE - WROWS - 16, COUT), jnp.bfloat16)
        eye = (
            lax.broadcasted_iota(jnp.int32, (COUT, COUT), 0)
            == lax.broadcasted_iota(jnp.int32, (COUT, COUT), 1)
        ).astype(jnp.bfloat16)

        we[shard(z, core), :] = lax.dot_general(
            eye, ext[...], (((1,), (1,)), ((), ())), preferred_element_type=jnp.float32
        ).astype(jnp.bfloat16)

    def first_copy(h, d):
        return pltpu.make_async_remote_copy(
            src_ref=lat.at[pl.ds(h * HALF, HALF)], dst_ref=near[h].at[place[h]],
            send_sem=s_lat.at[0, h, d - 1], recv_sem=r_lat.at[0, h, d - 1],
            device_id=(along(h, d), me_c), device_id_type=MESH,
        )

    def second_copy(h, d):
        return pltpu.make_async_remote_copy(
            src_ref=far_out.at[h, d - 1], dst_ref=far_in[h].at[place[1 - h]],
            send_sem=s_lat.at[1, h, d - 1], recv_sem=r_lat.at[1, h, d - 1],
            device_id=(along(1 - h, d), me_c), device_id_type=MESH,
        )

    def wanted(slot):
        own = assign[slot]
        return own, jnp.maximum(own - 1, 0)

    def spot(axis, tile):
        return tile % SIDE if axis == 0 else tile // SIDE

    def z_copy(d):
        rows = shard(z, core)
        return pltpu.make_async_remote_copy(
            src_ref=we.at[rows], dst_ref=we.at[rows],
            send_sem=s_z.at[d - 1], recv_sem=r_z.at[d - 1],
            device_id=(me_t, ((z + d) % zs) * 2 + core), device_id_type=MESH,
        )

    def sib_copy(d):
        rows = shard((z + zs - d) % zs, core)
        return pltpu.make_async_remote_copy(
            src_ref=we.at[rows], dst_ref=we.at[rows],
            send_sem=s_sib.at[d], recv_sem=r_sib.at[d],
            device_id=sibling, device_id_type=MESH,
        )

    def other(i):
        return i + (i >= z).astype(jnp.int32)

    def send_own():
        for i in range(zs - 1):
            z_copy((other(i) - z + zs) % zs).start()
        sib_copy(0).start()

    def hand_on():
        for i in range(zs - 1):
            d = (z - other(i) + zs) % zs
            z_copy(d).wait_recv()
            sib_copy(d).start()

    def finish_weights():
        for d in range(zs):
            sib_copy(d).wait_recv()

    sel_copy = pltpu.make_async_remote_copy(
        src_ref=sel, dst_ref=sel, send_sem=s_sel, recv_sem=r_sel, device_id=sibling, device_id_type=MESH,
    )
    order = (2, 1, zs - 1)
    turns = (2, 1, SIDE - 1)

    @pl.when(core == 0)
    def _():
        def meet():
            pl.semaphore_wait(barrier, chans - 1)
            pl.semaphore_signal(ready, inc=1, device_id=sibling, device_id_type=MESH)

        @pl.when(z < LATE)
        def _():
            pack_weights()
            meet()

        @pl.when(z >= LATE)
        def _():
            meet()
            pack_weights()

        send_own()
        prepare_rest()
        hand_on()
        finish_weights()
        sel_copy.wait_recv()

    @pl.when(core == 1)
    def _():
        for copy in own_copies:
            copy.start()

        def send_weights():
            pl.semaphore_wait(ready, 1)
            send_own()

        def send_latents():
            pl.semaphore_wait(barrier, 2 * (SIDE - 1))
            for d in turns:
                for h in range(2):
                    first_copy(h, d).start()

        first = z < EARLY

        @pl.when(first)
        def _():
            send_latents()
            pack_weights()
            send_weights()

        @pl.when(jnp.logical_not(first))
        def _():
            pack_weights()
            send_weights()
            send_latents()

        prepare_rest()
        for copy in own_copies:
            copy.wait()
        for h in range(2):
            for d in turns:
                first_copy(h, d).wait_recv()
            for d in turns:
                for j, tile in enumerate(wanted(along(1 - h, d))):
                    far_out[h, d - 1, j] = near[h][spot(h, tile)]
                second_copy(h, d).start()
            for j, tile in enumerate(wanted(me_t)):
                far_in[h][place[1 - h], j] = near[h][spot(h, tile)]
        for h in range(2):
            for d in turns:
                second_copy(h, d).wait_recv()
            for j, tile in enumerate(wanted(me_t)):
                sel[j, h * HALF:(h + 1) * HALF] = far_in[h][spot(1 - h, tile), j]
        sel_copy.start()
        hand_on()
        finish_weights()

    def drain():
        for d in order:
            z_copy(d).wait_send()
        for d in range(zs):
            sib_copy(d).wait_send()

        @pl.when(core == 1)
        def _():
            for h in range(2):
                for d in turns:
                    first_copy(h, d).wait_send()
                    second_copy(h, d).wait_send()
            sel_copy.wait_send()

    return drain


def decode_kernel(
    w_copies, durations, assign, we, sel, params,
    out, wm, flat, xe, entry, xp, prod, fine, tails, spread, permute,
):
    f32, bf16 = jnp.float32, jnp.bfloat16
    lane = lax.broadcasted_iota(jnp.int32, (1, CELLS), 1)
    cell_r, cell_q = lane // WT, lane % WT
    diagonal = lax.broadcasted_iota(jnp.int32, (COUT, COUT), 0) == lax.broadcasted_iota(jnp.int32, (COUT, COUT), 1)

    def column(ref):
        return jnp.sum(jnp.where(diagonal, ref, 0.0), axis=1, keepdims=True)

    bias_col, gain_col, shift_col = (column(params[n]) for n in range(3, 6))
    own = assign[lax.axis_index("tile")]
    duration_of = (durations[own], durations[jnp.maximum(own - 1, 0)])
    groups = COUT // GSIZE

    def frame(f):
        return slice(f * CELLS, (f + 1) * CELLS)

    def add_live(terms, duration):
        total = terms[0]
        for f in range(1, FT):
            total = total + (terms[f] if f < FT // 2 else terms[f] * (f < duration).astype(f32))
        return total

    def im2col(j):
        flat[...] = sel[j].astype(f32).reshape(CL * FT, CELLS)
        base = jnp.concatenate([flat[pl.ds(f, CL, stride=FT), :] for f in range(FT)], axis=0)
        for s in range(9):
            b, c = s // 3 - 1, s % 3 - 1
            moved = base
            if s != 4:
                moved = pltpu.roll(base, (-(b * WT + c)) % CELLS, 1)
                inside = (cell_r + b >= 0) & (cell_r + b < CELLS // WT) & (cell_q + c >= 0) & (cell_q + c < WT)
                moved = jnp.where(inside, moved, 0.0)
            moved = moved.astype(bf16)
            for a in range(3):
                for f in range(FT):
                    at = max(f - 2 + a, 0)
                    xe[j, (9 * a + s) * CL:(9 * a + s + 1) * CL, frame(f)] = moved[at * CL:(at + 1) * CL]

    chunks = [slice(i * COUT, (i + 1) * COUT) for i in range(CIN // COUT)]
    pairs = range(FT // 2)

    def pair(n):
        return slice(n * 2 * CELLS, (n + 1) * 2 * CELLS)

    def enter(j, n):
        entry[j, :, pair(n)] = jnp.dot(we[...], xe[j, :, pair(n)], preferred_element_type=f32)

    def group_sum(x, members):
        return jnp.sum(x.reshape(groups, GSIZE, CELLS), axis=(1, 2), keepdims=True) * members

    def spread_rows(x):
        return jnp.broadcast_to(x, (groups, GSIZE, 1)).reshape(COUT, 1)

    means, scales, coefs = {}, {}, {}
    members = [1.0 / (GSIZE * CELLS * d.astype(f32)) for d in duration_of]

    def mean_of(j, i):
        total = add_live([entry[j, chunks[i], frame(f)] for f in range(FT)], duration_of[j])
        means[j, i] = spread_rows(group_sum(total, members[j]))

    def scale_of(j, i):
        squares = []
        for f in range(FT):
            centred = entry[j, chunks[i], frame(f)] - means[j, i]
            squares.append(centred * centred)
        var = group_sum(add_live(squares, duration_of[j]), members[j])
        scales[j, i] = spread_rows(0.5 * lax.rsqrt(var + EPS))

    def coef_of(i):
        start = WROWS + 3 - (KE - CELLS)
        extra = we[chunks[i], KE - CELLS:].astype(f32)
        g1 = jnp.sum(jnp.where((lane >= start) & (lane < start + 3), extra, 0.0), axis=1, keepdims=True)
        b1 = jnp.sum(jnp.where((lane >= start + 3) & (lane < start + 6), extra, 0.0), axis=1, keepdims=True)
        coefs[i] = g1, b1

    def normalise(j, n):
        for i, at in enumerate(chunks):
            g1, b1 = coefs[i]
            scale = scales[j, i] * g1
            offset = 0.5 * b1 - means[j, i] * scale
            for f in (2 * n, 2 * n + 1):
                half = entry[j, at, frame(f)] * scale + offset
                coarse = (half * jnp.tanh(half) + half).astype(bf16)
                xp[j, at, frame(f + 2)] = coarse
                if f == 0:
                    xp[j, at, frame(0)] = coarse
                    xp[j, at, frame(1)] = coarse

    top, bottom = cell_r >= 1, cell_r < CELLS // WT - 1
    left, right = cell_q >= 1, cell_q < WT - 1

    def mix(j, n):
        first = n * 2 * CELLS
        delayed = jnp.concatenate(
            [xp[j, :, first + a * CELLS:first + (a + 2) * CELLS] for a in range(3)], axis=0
        )
        prod[j, :, pair(n)] = jnp.dot(wm[...], delayed, preferred_element_type=f32)

    sums, squares, pivots = {}, {}, {}

    def upsample(j, n):
        for f in (2 * n, 2 * n + 1):
            p = [prod[j, s * COUT:(s + 1) * COUT, frame(f)] for s in range(9)]
            p[4] = p[4] + bias_col
            upper, lower = [], []
            for c in range(3):
                upper.append(jnp.where(top, pltpu.roll(p[c], WT, 1), 0.0) + (p[3 + c] + p[6 + c]))
                lower.append((p[c] + p[3 + c]) + jnp.where(bottom, pltpu.roll(p[6 + c], CELLS - WT, 1), 0.0))
            phases = []
            for r in (upper, lower):
                phases.append(jnp.where(left, pltpu.roll(r[0], 1, 1), 0.0) + (r[1] + r[2]))
                phases.append((r[0] + r[1]) + jnp.where(right, pltpu.roll(r[2], CELLS - 1, 1), 0.0))
            for m in range(4):
                fine[j, f, :, frame(m)] = phases[m]
            sums[j, f] = (phases[0] + phases[1]) + (phases[2] + phases[3])
        if n == 0:
            pivots[j] = spread_rows(group_sum(sums[j, 0] + sums[j, 1], 1.0 / (GSIZE * 8 * CELLS)))
        for f in (2 * n, 2 * n + 1):
            total = None
            for m in range(4):
                apart = fine[j, f, :, frame(m)] - pivots[j]
                total = apart * apart if total is None else total + apart * apart
            squares[j, f] = total

    def finisher(j):
        members = 1.0 / (GSIZE * 4 * CELLS * duration_of[j].astype(f32))
        mean = group_sum(add_live([sums[j, f] for f in range(FT)], duration_of[j]), members)
        about = group_sum(add_live([squares[j, f] for f in range(FT)], duration_of[j]), members)
        mean = spread_rows(mean)
        off = mean - pivots[j]
        var = jnp.maximum(spread_rows(about) - off * off, 0.0)
        scale = gain_col * (0.5 * lax.rsqrt(var + EPS))
        offset = 0.5 * shift_col - mean * scale

        def finish(f, at=slice(None)):
            half = fine[j, f, at] * scale[at] + offset[at]
            return (half * jnp.tanh(half) + half).astype(bf16)

        return finish

    im2col(1)
    im2col(0)
    for n in pairs:
        enter(1, n)
    for i in range(len(chunks)):
        mean_of(1, i)
        coef_of(i)
        if i % 2:
            enter(0, i // 2)
    for i in range(len(chunks)):
        scale_of(1, i)
    normalise(1, 0)
    for copy in w_copies:
        copy.wait()
    for n in pairs:
        mix(1, n)
        if n + 1 < len(pairs):
            normalise(1, n + 1)
        for i in (2 * n, 2 * n + 1):
            mean_of(0, i)
        if n > 0:
            upsample(1, n - 1)
    for i in range(len(chunks)):
        scale_of(0, i)
    normalise(0, 0)
    for n in pairs:
        mix(0, n)
        if n + 1 < len(pairs):
            normalise(0, n + 1)
        if n == 0:
            upsample(1, len(pairs) - 1)
        if n == 1:
            finish = finisher(1)
            for k in range(OV):
                tails[k] = finish(jnp.clip(duration_of[1] - OV + k, 0, FT - 1))
        if n > 0:
            upsample(0, n - 1)
    upsample(0, len(pairs) - 1)
    finish = finisher(0)
    part = COUT // 2
    for at in (slice(0, part), slice(part, COUT)):
        for f in range(FT):
            result = finish(f, at).astype(f32)
            if f >= FT // 2:
                result = jnp.where(f < duration_of[0], result, 0.0)
            if f < OV:
                w = (f + 1) / (OV + 1)
                blended = result * w + tails[f, at].astype(f32) * (1.0 - w)
                result = jnp.where(own == 0, result, blended)
            for n in range(4):
                spread[n, pl.ds(at.start * FT + f, part, stride=FT), :] = result[:, frame(n)]
        whole = slice(at.start * FT, at.stop * FT)
        rows = jnp.concatenate([spread[n, whole, :].astype(bf16) for n in range(4)], axis=1)
        moved = jnp.dot(rows, permute[...], preferred_element_type=f32)
        out[at] = moved.astype(bf16).reshape(part, FT, 4 * CELLS)


def prepare(xe, permute):
    last = lax.broadcasted_iota(jnp.int32, (KE - WROWS, FT * CELLS), 0)
    ones = jnp.where(last < 3, 1.0, 0.0).astype(jnp.bfloat16)
    for j in range(2):
        xe[j, WROWS:, :] = ones
    col = lax.broadcasted_iota(jnp.int32, (1, 4 * CELLS), 1)
    fr, fc = col // (2 * WT), col % (2 * WT)
    source = ((fr % 2) * 2 + fc % 2) * CELLS + (fr // 2) * WT + fc // 2
    found = lax.broadcasted_iota(jnp.int32, (4 * CELLS, 4 * CELLS), 0) == source
    permute[...] = found.astype(jnp.float32).astype(jnp.bfloat16)


def fused_kernel(
    tiles, chans,
    durations_in, assign_in, lat, wt, bias1, gain1, shift1, w3, bias2, gain2, shift2,
    out,
    durations, assign, params, we, sel, ext, near0, near1, far_out, far_in0, far_in1,
    wm, flat, xe, entry, xp, prod, fine, tails, spread, permute,
    s_lat, r_lat, s_z, r_z, s_sib, r_sib, s_sel, r_sel, ready, w_sem, load_sem,
):
    me_t = lax.axis_index("tile")
    loads = [pltpu.make_async_copy(wt, ext.at[:WROWS], load_sem.at[0])]
    for n, ref in enumerate((bias1, gain1, shift1, bias2, gain2, shift2)):
        loads.append(pltpu.make_async_copy(ref, params.at[n], load_sem.at[n + 1]))
    loads.append(pltpu.make_async_copy(durations_in, durations, load_sem.at[7]))
    loads.append(pltpu.make_async_copy(assign_in, assign, load_sem.at[8]))
    near, far_in = (near0, near1), (far_in0, far_in1)
    own_copies = [
        pltpu.make_async_copy(lat.at[pl.ds(h * HALF, HALF)], near[h].at[place], load_sem.at[9 + h])
        for h, place in enumerate((me_t % SIDE, me_t // SIDE))
    ]
    w_copies = [
        pltpu.make_async_copy(w3.at[a], wm.at[:, a * CIN:(a + 1) * CIN], w_sem.at[a]) for a in range(3)
    ]

    def start_loads():
        for copy in loads + w_copies:
            copy.start()

    drain = gather_kernel(
        tiles, chans, lambda: prepare(xe, permute), start_loads, loads, own_copies, assign, lat, params, we, sel, ext,
        near, far_out, far_in,
        s_lat, r_lat, s_z, r_z, s_sib, r_sib, s_sel, r_sel, ready,
    )
    decode_kernel(
        w_copies, durations, assign, we, sel, params,
        out, wm, flat, xe, entry, xp, prod, fine, tails, spread, permute,
    )
    drain()


def fused(tiles, chans, *args):
    vmem = pl.BlockSpec(memory_space=pltpu.VMEM)
    hbm = pl.BlockSpec(memory_space=pl.ANY)
    dma = pltpu.SemaphoreType.DMA
    bf16, f32 = jnp.bfloat16, jnp.float32
    return pl.pallas_call(
        functools.partial(fused_kernel, tiles, chans),
        out_shape=pltpu.VMEM((COUT, FT, 4 * CELLS), bf16),
        in_specs=[hbm] * 11,
        out_specs=vmem,
        scratch_shapes=[
            pltpu.SMEM((tiles,), jnp.int32),
            pltpu.SMEM((tiles,), jnp.int32),
            pltpu.VMEM((6, 1, COUT), f32),
            pltpu.VMEM((CIN, KE), bf16),
            pltpu.VMEM((2, CL, FT, CELLS), bf16),
            pltpu.VMEM((KE, COUT), bf16),
            *[pltpu.VMEM((SIDE, HALF, FT, CELLS), bf16)] * 2,
            pltpu.VMEM((2, SIDE - 1, 2, HALF, FT, CELLS), bf16),
            *[pltpu.VMEM((SIDE, 2, HALF, FT, CELLS), bf16)] * 2,
            pltpu.VMEM((9 * COUT, 3 * CIN), bf16),
            pltpu.VMEM((CL * FT, CELLS), f32),
            pltpu.VMEM((2, KE, FT * CELLS), bf16),
            pltpu.VMEM((2, CIN, FT * CELLS), f32),
            pltpu.VMEM((2, CIN, (FT + 2) * CELLS), bf16),
            pltpu.VMEM((2, 9 * COUT, FT * CELLS), f32),
            pltpu.VMEM((2, FT, COUT, 4 * CELLS), f32),
            pltpu.VMEM((OV, COUT, 4 * CELLS), bf16),
            pltpu.VMEM((4, FT * COUT, CELLS), f32),
            pltpu.VMEM((4 * CELLS, 4 * CELLS), bf16),
            dma((2, 2, SIDE - 1)), dma((2, 2, SIDE - 1)),
            dma((3,)), dma((3,)),
            dma((4,)), dma((4,)),
            dma, dma, pltpu.SemaphoreType.REGULAR,
            dma((3,)),
            dma((11,)),
        ],
        compiler_params=pltpu.CompilerParams(
            collective_id=0, has_side_effects=True, vmem_limit_bytes=56 * 1024 * 1024
        ),
    )(*args)


def solution(mesh):
    tiles, chans = mesh.shape["tile"], mesh.shape["chan"]

    def local(latents, durations, assignment, entry_weight, entry_bias, first_gain, first_shift,
              mixer_weight, mixer_bias, second_gain, second_shift):
        wt = jnp.transpose(entry_weight, (0, 2, 1)).reshape(WROWS, COUT)
        out = fused(
            tiles, chans, durations, assignment, latents[0], wt, entry_bias[None], first_gain[None],
            first_shift[None], mixer_weight.reshape(3, 9 * COUT, CIN), mixer_bias[None], second_gain[None],
            second_shift[None],
        )
        return out[None]

    in_specs = (
        P("tile", None, None, None), P(), P(), P(None, "chan", None), P("chan"), P("chan"), P("chan"),
        P(None, "chan", None), P("chan"), P("chan"), P("chan"),
    )
    return jax.shard_map(
        local, mesh=mesh, in_specs=in_specs, out_specs=P("tile", "chan", None, None), check_vma=False
    )
```

```python
import functools

import jax
import jax.numpy as jnp
from jax import lax
from jax.experimental import pallas as pl
from jax.experimental.pallas import tpu as pltpu
from jax.sharding import PartitionSpec as P

MESH = pl.DeviceIdType.MESH
GSIZE = 16
OV = 3
FT = 8
WT = 16
CELLS = 128
CL = 16
COUT = 64
CIN = 512
KE = 512
WROWS = 432
EARLY = 3
SIDE = 4
HALF = CL // 2
LATE = 0
EPS = 1e-06


def three_parts(x):
    hi = x.astype(jnp.bfloat16).astype(jnp.float32)
    rest = x - hi
    mid = rest.astype(jnp.bfloat16).astype(jnp.float32)
    return hi, mid, rest - mid


def gather_kernel(
    tiles, chans, prepare_rest, start_loads, loads, own_copies,
    assign, lat, params,
    we, sel,
    ext, near, far_out, far_in,
    s_lat, r_lat, s_z, r_z, s_sib, r_sib, s_sel, r_sel, ready,
):
    me_t = lax.axis_index("tile")
    me_c = lax.axis_index("chan")
    z, core = me_c // 2, me_c % 2
    zs = chans // 2
    sibling = (me_t, z * 2 + 1 - core)

    place = (me_t % SIDE, me_t // SIDE)

    def along(axis, d):
        x, y = place
        return y * SIDE + (x + d) % SIDE if axis == 0 else ((y + d) % SIDE) * SIDE + x

    barrier = pltpu.get_barrier_semaphore()

    @pl.when(core == 0)
    def _():
        for d in range(1, zs):
            pl.semaphore_signal(barrier, inc=1, device_id=(me_t, ((z + d) % zs) * 2), device_id_type=MESH)

    @pl.when(core == 1)
    def _():
        for d in range(zs):
            pl.semaphore_signal(barrier, inc=1, device_id=(me_t, ((z + d) % zs) * 2), device_id_type=MESH)
        for axis in range(2):
            for d in range(1, SIDE):
                pl.semaphore_signal(barrier, inc=1, device_id=(along(axis, d), me_c), device_id_type=MESH)

    start_loads()

    def shard(chip, half):
        return pl.ds(pl.multiple_of((chip * 2 + half) * COUT, COUT), COUT)

    def pack_weights():
        for copy in loads:
            copy.wait()
        row = lax.broadcasted_iota(jnp.int32, (16, COUT), 0)
        packed = jnp.zeros((16, COUT), jnp.float32)
        for n in range(3):
            for at, piece in enumerate(three_parts(params[n])):
                packed = jnp.where(row == 3 * n + at, piece, packed)
        ext[WROWS:WROWS + 16, :] = packed.astype(jnp.bfloat16)
        ext[WROWS + 16:, :] = jnp.zeros((KE - WROWS - 16, COUT), jnp.bfloat16)
        eye = (
            lax.broadcasted_iota(jnp.int32, (COUT, COUT), 0)
            == lax.broadcasted_iota(jnp.int32, (COUT, COUT), 1)
        ).astype(jnp.bfloat16)

        we[shard(z, core), :] = lax.dot_general(
            eye, ext[...], (((1,), (1,)), ((), ())), preferred_element_type=jnp.float32
        ).astype(jnp.bfloat16)

    def first_copy(h, d):
        return pltpu.make_async_remote_copy(
            src_ref=lat.at[pl.ds(h * HALF, HALF)], dst_ref=near[h].at[place[h]],
            send_sem=s_lat.at[0, h, d - 1], recv_sem=r_lat.at[0, h, d - 1],
            device_id=(along(h, d), me_c), device_id_type=MESH,
        )

    def second_copy(h, d):
        return pltpu.make_async_remote_copy(
            src_ref=far_out.at[h, d - 1], dst_ref=far_in[h].at[place[1 - h]],
            send_sem=s_lat.at[1, h, d - 1], recv_sem=r_lat.at[1, h, d - 1],
            device_id=(along(1 - h, d), me_c), device_id_type=MESH,
        )

    def wanted(slot):
        own = assign[slot]
        return own, jnp.maximum(own - 1, 0)

    def spot(axis, tile):
        return tile % SIDE if axis == 0 else tile // SIDE

    def z_copy(d):
        rows = shard(z, core)
        return pltpu.make_async_remote_copy(
            src_ref=we.at[rows], dst_ref=we.at[rows],
            send_sem=s_z.at[d - 1], recv_sem=r_z.at[d - 1],
            device_id=(me_t, ((z + d) % zs) * 2 + core), device_id_type=MESH,
        )

    def sib_copy(d):
        rows = shard((z + zs - d) % zs, core)
        return pltpu.make_async_remote_copy(
            src_ref=we.at[rows], dst_ref=we.at[rows],
            send_sem=s_sib.at[d], recv_sem=r_sib.at[d],
            device_id=sibling, device_id_type=MESH,
        )

    def other(i):
        return i + (i >= z).astype(jnp.int32)

    def send_own():
        for i in range(zs - 1):
            z_copy((other(i) - z + zs) % zs).start()
        sib_copy(0).start()

    def hand_on():
        for i in range(zs - 1):
            d = (z - other(i) + zs) % zs
            z_copy(d).wait_recv()
            sib_copy(d).start()

    def finish_weights():
        for d in range(zs):
            sib_copy(d).wait_recv()

    sel_copy = pltpu.make_async_remote_copy(
        src_ref=sel, dst_ref=sel, send_sem=s_sel, recv_sem=r_sel, device_id=sibling, device_id_type=MESH,
    )
    order = (2, 1, zs - 1)
    turns = (2, 1, SIDE - 1)

    @pl.when(core == 0)
    def _():
        def meet():
            pl.semaphore_wait(barrier, chans - 1)
            pl.semaphore_signal(ready, inc=1, device_id=sibling, device_id_type=MESH)

        @pl.when(z < LATE)
        def _():
            pack_weights()
            meet()

        @pl.when(z >= LATE)
        def _():
            meet()
            pack_weights()

        send_own()
        prepare_rest()
        hand_on()
        finish_weights()
        sel_copy.wait_recv()

    @pl.when(core == 1)
    def _():
        for copy in own_copies:
            copy.start()

        def send_weights():
            pl.semaphore_wait(ready, 1)
            send_own()

        def send_latents():
            pl.semaphore_wait(barrier, 2 * (SIDE - 1))
            for d in turns:
                for h in range(2):
                    first_copy(h, d).start()

        first = z < EARLY

        @pl.when(first)
        def _():
            pack_weights()
            send_latents()
            send_weights()

        @pl.when(jnp.logical_not(first))
        def _():
            pack_weights()
            send_weights()
            send_latents()

        prepare_rest()
        for copy in own_copies:
            copy.wait()
        for h in range(2):
            for d in turns:
                first_copy(h, d).wait_recv()
            for d in turns:
                for j, tile in enumerate(wanted(along(1 - h, d))):
                    far_out[h, d - 1, j] = near[h][spot(h, tile)]
                second_copy(h, d).start()
            for j, tile in enumerate(wanted(me_t)):
                far_in[h][place[1 - h], j] = near[h][spot(h, tile)]
        for h in range(2):
            for d in turns:
                second_copy(h, d).wait_recv()
            for j, tile in enumerate(wanted(me_t)):
                sel[j, h * HALF:(h + 1) * HALF] = far_in[h][spot(1 - h, tile), j]
        sel_copy.start()
        hand_on()
        finish_weights()

    def drain():
        for d in order:
            z_copy(d).wait_send()
        for d in range(zs):
            sib_copy(d).wait_send()

        @pl.when(core == 1)
        def _():
            for h in range(2):
                for d in turns:
                    first_copy(h, d).wait_send()
                    second_copy(h, d).wait_send()
            sel_copy.wait_send()

    return drain


def decode_kernel(
    w_copies, durations, assign, we, sel, params,
    out, wm, flat, xe, entry, xp, prod, fine, tails, spread, permute,
):
    f32, bf16 = jnp.float32, jnp.bfloat16
    lane = lax.broadcasted_iota(jnp.int32, (1, CELLS), 1)
    cell_r, cell_q = lane // WT, lane % WT
    diagonal = lax.broadcasted_iota(jnp.int32, (COUT, COUT), 0) == lax.broadcasted_iota(jnp.int32, (COUT, COUT), 1)

    def column(ref):
        return jnp.sum(jnp.where(diagonal, ref, 0.0), axis=1, keepdims=True)

    bias_col, gain_col, shift_col = (column(params[n]) for n in range(3, 6))
    own = assign[lax.axis_index("tile")]
    duration_of = (durations[own], durations[jnp.maximum(own - 1, 0)])
    groups = COUT // GSIZE

    def frame(f):
        return slice(f * CELLS, (f + 1) * CELLS)

    def add_live(terms, duration):
        total = terms[0]
        for f in range(1, FT):
            total = total + (terms[f] if f < FT // 2 else terms[f] * (f < duration).astype(f32))
        return total

    def im2col(j):
        flat[...] = sel[j].astype(f32).reshape(CL * FT, CELLS)
        base = jnp.concatenate([flat[pl.ds(f, CL, stride=FT), :] for f in range(FT)], axis=0)
        for s in range(9):
            b, c = s // 3 - 1, s % 3 - 1
            moved = base
            if s != 4:
                moved = pltpu.roll(base, (-(b * WT + c)) % CELLS, 1)
                inside = (cell_r + b >= 0) & (cell_r + b < CELLS // WT) & (cell_q + c >= 0) & (cell_q + c < WT)
                moved = jnp.where(inside, moved, 0.0)
            moved = moved.astype(bf16)
            for a in range(3):
                for f in range(FT):
                    at = max(f - 2 + a, 0)
                    xe[j, (9 * a + s) * CL:(9 * a + s + 1) * CL, frame(f)] = moved[at * CL:(at + 1) * CL]

    chunks = [slice(i * COUT, (i + 1) * COUT) for i in range(CIN // COUT)]
    pairs = range(FT // 2)

    def pair(n):
        return slice(n * 2 * CELLS, (n + 1) * 2 * CELLS)

    def enter(j, n):
        entry[j, :, pair(n)] = jnp.dot(we[...], xe[j, :, pair(n)], preferred_element_type=f32)

    def group_sum(x, members):
        return jnp.sum(x.reshape(groups, GSIZE, CELLS), axis=(1, 2), keepdims=True) * members

    def spread_rows(x):
        return jnp.broadcast_to(x, (groups, GSIZE, 1)).reshape(COUT, 1)

    means, scales, coefs = {}, {}, {}
    members = [1.0 / (GSIZE * CELLS * d.astype(f32)) for d in duration_of]

    def mean_of(j, i):
        total = add_live([entry[j, chunks[i], frame(f)] for f in range(FT)], duration_of[j])
        means[j, i] = spread_rows(group_sum(total, members[j]))

    def scale_of(j, i):
        squares = []
        for f in range(FT):
            centred = entry[j, chunks[i], frame(f)] - means[j, i]
            squares.append(centred * centred)
        var = group_sum(add_live(squares, duration_of[j]), members[j])
        scales[j, i] = spread_rows(0.5 * lax.rsqrt(var + EPS))

    def coef_of(i):
        start = WROWS + 3 - (KE - CELLS)
        extra = we[chunks[i], KE - CELLS:].astype(f32)
        g1 = jnp.sum(jnp.where((lane >= start) & (lane < start + 3), extra, 0.0), axis=1, keepdims=True)
        b1 = jnp.sum(jnp.where((lane >= start + 3) & (lane < start + 6), extra, 0.0), axis=1, keepdims=True)
        coefs[i] = g1, b1

    def normalise(j, n):
        for i, at in enumerate(chunks):
            g1, b1 = coefs[i]
            scale = scales[j, i] * g1
            offset = 0.5 * b1 - means[j, i] * scale
            for f in (2 * n, 2 * n + 1):
                half = entry[j, at, frame(f)] * scale + offset
                coarse = (half * jnp.tanh(half) + half).astype(bf16)
                xp[j, at, frame(f + 2)] = coarse
                if f == 0:
                    xp[j, at, frame(0)] = coarse
                    xp[j, at, frame(1)] = coarse

    top, bottom = cell_r >= 1, cell_r < CELLS // WT - 1
    left, right = cell_q >= 1, cell_q < WT - 1

    def mix(j, n):
        first = n * 2 * CELLS
        delayed = jnp.concatenate(
            [xp[j, :, first + a * CELLS:first + (a + 2) * CELLS] for a in range(3)], axis=0
        )
        prod[j, :, pair(n)] = jnp.dot(wm[...], delayed, preferred_element_type=f32)

    sums, squares, pivots = {}, {}, {}

    def upsample(j, n):
        for f in (2 * n, 2 * n + 1):
            p = [prod[j, s * COUT:(s + 1) * COUT, frame(f)] for s in range(9)]
            p[4] = p[4] + bias_col
            upper, lower = [], []
            for c in range(3):
                upper.append(jnp.where(top, pltpu.roll(p[c], WT, 1), 0.0) + (p[3 + c] + p[6 + c]))
                lower.append((p[c] + p[3 + c]) + jnp.where(bottom, pltpu.roll(p[6 + c], CELLS - WT, 1), 0.0))
            phases = []
            for r in (upper, lower):
                phases.append(jnp.where(left, pltpu.roll(r[0], 1, 1), 0.0) + (r[1] + r[2]))
                phases.append((r[0] + r[1]) + jnp.where(right, pltpu.roll(r[2], CELLS - 1, 1), 0.0))
            for m in range(4):
                fine[j, f, :, frame(m)] = phases[m]
            sums[j, f] = (phases[0] + phases[1]) + (phases[2] + phases[3])
        if n == 0:
            pivots[j] = spread_rows(group_sum(sums[j, 0] + sums[j, 1], 1.0 / (GSIZE * 8 * CELLS)))
        for f in (2 * n, 2 * n + 1):
            total = None
            for m in range(4):
                apart = fine[j, f, :, frame(m)] - pivots[j]
                total = apart * apart if total is None else total + apart * apart
            squares[j, f] = total

    def finisher(j):
        members = 1.0 / (GSIZE * 4 * CELLS * duration_of[j].astype(f32))
        mean = group_sum(add_live([sums[j, f] for f in range(FT)], duration_of[j]), members)
        about = group_sum(add_live([squares[j, f] for f in range(FT)], duration_of[j]), members)
        mean = spread_rows(mean)
        off = mean - pivots[j]
        var = jnp.maximum(spread_rows(about) - off * off, 0.0)
        scale = gain_col * (0.5 * lax.rsqrt(var + EPS))
        offset = 0.5 * shift_col - mean * scale

        def finish(f, at=slice(None)):
            half = fine[j, f, at] * scale[at] + offset[at]
            return (half * jnp.tanh(half) + half).astype(bf16)

        return finish

    im2col(1)
    im2col(0)
    for n in pairs:
        enter(1, n)
    for i in range(len(chunks)):
        mean_of(1, i)
        coef_of(i)
        if i % 2:
            enter(0, i // 2)
    for i in range(len(chunks)):
        scale_of(1, i)
    normalise(1, 0)
    for copy in w_copies:
        copy.wait()
    for n in pairs:
        mix(1, n)
        if n + 1 < len(pairs):
            normalise(1, n + 1)
        for i in (2 * n, 2 * n + 1):
            mean_of(0, i)
        if n > 0:
            upsample(1, n - 1)
    for i in range(len(chunks)):
        scale_of(0, i)
    normalise(0, 0)
    for n in pairs:
        mix(0, n)
        if n + 1 < len(pairs):
            normalise(0, n + 1)
        if n == 0:
            upsample(1, len(pairs) - 1)
        if n == 1:
            finish = finisher(1)
            for k in range(OV):
                tails[k] = finish(jnp.clip(duration_of[1] - OV + k, 0, FT - 1))
        if n > 0:
            upsample(0, n - 1)
    upsample(0, len(pairs) - 1)
    finish = finisher(0)
    part = COUT // 2
    for at in (slice(0, part), slice(part, COUT)):
        for f in range(FT):
            result = finish(f, at).astype(f32)
            if f >= FT // 2:
                result = jnp.where(f < duration_of[0], result, 0.0)
            if f < OV:
                w = (f + 1) / (OV + 1)
                blended = result * w + tails[f, at].astype(f32) * (1.0 - w)
                result = jnp.where(own == 0, result, blended)
            for n in range(4):
                spread[n, pl.ds(at.start * FT + f, part, stride=FT), :] = result[:, frame(n)]
        whole = slice(at.start * FT, at.stop * FT)
        rows = jnp.concatenate([spread[n, whole, :].astype(bf16) for n in range(4)], axis=1)
        moved = jnp.dot(rows, permute[...], preferred_element_type=f32)
        out[at] = moved.astype(bf16).reshape(part, FT, 4 * CELLS)


def prepare(xe, permute):
    last = lax.broadcasted_iota(jnp.int32, (KE - WROWS, FT * CELLS), 0)
    ones = jnp.where(last < 3, 1.0, 0.0).astype(jnp.bfloat16)
    for j in range(2):
        xe[j, WROWS:, :] = ones
    col = lax.broadcasted_iota(jnp.int32, (1, 4 * CELLS), 1)
    fr, fc = col // (2 * WT), col % (2 * WT)
    source = ((fr % 2) * 2 + fc % 2) * CELLS + (fr // 2) * WT + fc // 2
    found = lax.broadcasted_iota(jnp.int32, (4 * CELLS, 4 * CELLS), 0) == source
    permute[...] = found.astype(jnp.float32).astype(jnp.bfloat16)


def fused_kernel(
    tiles, chans,
    durations_in, assign_in, lat, wt, bias1, gain1, shift1, w3, bias2, gain2, shift2,
    out,
    durations, assign, params, we, sel, ext, near0, near1, far_out, far_in0, far_in1,
    wm, flat, xe, entry, xp, prod, fine, tails, spread, permute,
    s_lat, r_lat, s_z, r_z, s_sib, r_sib, s_sel, r_sel, ready, w_sem, load_sem,
):
    me_t = lax.axis_index("tile")
    loads = [pltpu.make_async_copy(wt, ext.at[:WROWS], load_sem.at[0])]
    for n, ref in enumerate((bias1, gain1, shift1, bias2, gain2, shift2)):
        loads.append(pltpu.make_async_copy(ref, params.at[n], load_sem.at[n + 1]))
    loads.append(pltpu.make_async_copy(durations_in, durations, load_sem.at[7]))
    loads.append(pltpu.make_async_copy(assign_in, assign, load_sem.at[8]))
    near, far_in = (near0, near1), (far_in0, far_in1)
    own_copies = [
        pltpu.make_async_copy(lat.at[pl.ds(h * HALF, HALF)], near[h].at[place], load_sem.at[9 + h])
        for h, place in enumerate((me_t % SIDE, me_t // SIDE))
    ]
    w_copies = [
        pltpu.make_async_copy(w3.at[a], wm.at[:, a * CIN:(a + 1) * CIN], w_sem.at[a]) for a in range(3)
    ]

    def start_loads():
        for copy in loads + w_copies:
            copy.start()

    drain = gather_kernel(
        tiles, chans, lambda: prepare(xe, permute), start_loads, loads, own_copies, assign, lat, params, we, sel, ext,
        near, far_out, far_in,
        s_lat, r_lat, s_z, r_z, s_sib, r_sib, s_sel, r_sel, ready,
    )
    decode_kernel(
        w_copies, durations, assign, we, sel, params,
        out, wm, flat, xe, entry, xp, prod, fine, tails, spread, permute,
    )
    drain()


def fused(tiles, chans, *args):
    vmem = pl.BlockSpec(memory_space=pltpu.VMEM)
    hbm = pl.BlockSpec(memory_space=pl.ANY)
    dma = pltpu.SemaphoreType.DMA
    bf16, f32 = jnp.bfloat16, jnp.float32
    return pl.pallas_call(
        functools.partial(fused_kernel, tiles, chans),
        out_shape=pltpu.VMEM((COUT, FT, 4 * CELLS), bf16),
        in_specs=[hbm] * 11,
        out_specs=vmem,
        scratch_shapes=[
            pltpu.SMEM((tiles,), jnp.int32),
            pltpu.SMEM((tiles,), jnp.int32),
            pltpu.VMEM((6, 1, COUT), f32),
            pltpu.VMEM((CIN, KE), bf16),
            pltpu.VMEM((2, CL, FT, CELLS), bf16),
            pltpu.VMEM((KE, COUT), bf16),
            *[pltpu.VMEM((SIDE, HALF, FT, CELLS), bf16)] * 2,
            pltpu.VMEM((2, SIDE - 1, 2, HALF, FT, CELLS), bf16),
            *[pltpu.VMEM((SIDE, 2, HALF, FT, CELLS), bf16)] * 2,
            pltpu.VMEM((9 * COUT, 3 * CIN), bf16),
            pltpu.VMEM((CL * FT, CELLS), f32),
            pltpu.VMEM((2, KE, FT * CELLS), bf16),
            pltpu.VMEM((2, CIN, FT * CELLS), f32),
            pltpu.VMEM((2, CIN, (FT + 2) * CELLS), bf16),
            pltpu.VMEM((2, 9 * COUT, FT * CELLS), f32),
            pltpu.VMEM((2, FT, COUT, 4 * CELLS), f32),
            pltpu.VMEM((OV, COUT, 4 * CELLS), bf16),
            pltpu.VMEM((4, FT * COUT, CELLS), f32),
            pltpu.VMEM((4 * CELLS, 4 * CELLS), bf16),
            dma((2, 2, SIDE - 1)), dma((2, 2, SIDE - 1)),
            dma((3,)), dma((3,)),
            dma((4,)), dma((4,)),
            dma, dma, pltpu.SemaphoreType.REGULAR,
            dma((3,)),
            dma((11,)),
        ],
        compiler_params=pltpu.CompilerParams(
            collective_id=0, has_side_effects=True, vmem_limit_bytes=56 * 1024 * 1024
        ),
    )(*args)


def solution(mesh):
    tiles, chans = mesh.shape["tile"], mesh.shape["chan"]

    def local(latents, durations, assignment, entry_weight, entry_bias, first_gain, first_shift,
              mixer_weight, mixer_bias, second_gain, second_shift):
        wt = jnp.transpose(entry_weight, (0, 2, 1)).reshape(WROWS, COUT)
        out = fused(
            tiles, chans, durations, assignment, latents[0], wt, entry_bias[None], first_gain[None],
            first_shift[None], mixer_weight.reshape(3, 9 * COUT, CIN), mixer_bias[None], second_gain[None],
            second_shift[None],
        )
        return out[None]

    in_specs = (
        P("tile", None, None, None), P(), P(), P(None, "chan", None), P("chan"), P("chan"), P("chan"),
        P(None, "chan", None), P("chan"), P("chan"), P("chan"),
    )
    return jax.shard_map(
        local, mesh=mesh, in_specs=in_specs, out_specs=P("tile", "chan", None, None), check_vma=False
    )
```
